32 devices in a mesh: row: 4 (over y, x), col: 8 (over z, core).
Axes of the slice: x: 2, y: 2, z: 4, core: 2. Of those that a mesh axis runs over, the one named last changes fastest.
Arguments:
- bricks: bfloat16 [4, 8, 2, 16, 128, 128], P('row', 'col'), may hold values from -98304 to 98304
- brick_coords: int32 [4, 8, 3, 2], P('row', 'col'), may hold values from 0 to 31, as said below
- brick_counts: int32 [4, 8], P('row', 'col'), may hold values from 0 to 2, as said below
- step_sizes: float32 [2, 3], replicated, may hold values from 0.3 to 1
- init_a: float32 [4, 512, 256], P('row', 'col'), may hold values from -6 to 6
- init_b: float32 [8, 256, 256], P('col', 'row'), may hold values from -6 to 6
- init_c: float32 [512, 256], replicated, may hold values from -6 to 6
Outputs:
- factor_a: float32 [4, 512, 256], P('row', 'col')
- factor_b: float32 [8, 256, 256], P('col', 'row')
- factor_c: float32 [512, 256], replicated
The draws below stay inside these ranges and needn't reach their ends.
Inputs may be any that keep to these rules, and one draw needn't show every extreme that they name: brick_counts of rows r and (r + half of the row axis) mod the row axis in one column add up to at most 3; some device holds 2 bricks. `brick_coords`: component 0 is below 4, component 1 below 2, component 2 below 32; dead slots hold arbitrary positions.
All inputs are finite; a program needn't handle non-finite values.
Results may differ from the reference program's by a relative error of at most 0.0003.
The reference program's roundings to bfloat16 on the way count: a program that leaves them out, or rounds other values in their place, can miss the bound.
Values may be sent and summed in bfloat16 or wider, within the bound.
A program may use at most 64 MiB of HBM per device.

```python
import math
import jax
import jax.numpy as jnp
from jax import lax

R = 256
TILE = 128
BK = 16
TI = 4
TJ = 2
KT = 32
MAXB = 2
SWEEPS = 2
J = 2048
K = 512
N_ROW = 4
N_COL = 8


def draw_brick_counts(key, part):
    half = N_ROW // 2
    keys = jax.random.split(key, 5)
    total = jax.random.randint(keys[0], (half, N_COL), 0, MAXB + 2)
    forced_row = jax.random.randint(keys[1], (), 0, half)
    forced_col = jax.random.randint(keys[2], (), 0, N_COL)
    hit = (jnp.arange(half)[:, None] == forced_row) & (jnp.arange(N_COL)[None, :] == forced_col)
    total = jnp.where(hit, MAXB + 1, total)
    low = jnp.maximum(total - MAXB, 0)
    high = jnp.minimum(total, MAXB)
    first = jax.random.randint(keys[3], (half, N_COL), low, high + 1)
    first = jnp.where(hit, MAXB, first)
    second = total - first
    flip = jax.random.randint(keys[4], (half, N_COL), 0, 2)
    upper = jnp.where(flip == 1, first, second)
    lower = total - upper
    return jnp.concatenate([upper, lower], axis=0).astype(jnp.int32)


def draw_brick_coords(key, part):
    keys = jax.random.split(key, 3)
    shape = (N_ROW, N_COL, 1, MAXB)
    first = jax.random.randint(keys[0], shape, 0, TI)
    second = jax.random.randint(keys[1], shape, 0, TJ)
    third = jax.random.randint(keys[2], shape, 0, KT)
    return jnp.concatenate([first, second, third], axis=2).astype(jnp.int32)


def shard_levels(own_key, dims, shards, least, top_value):
    gain, own = 1.0, jax.random.fold_in(own_key, 6)
    for axis_at, blocks in shards:
        steps = jnp.exp(jax.random.uniform(jax.random.fold_in(own, axis_at), (blocks,), jnp.float32, least / len(shards), top_value / len(shards)))
        gain = gain * jnp.repeat(steps, dims[axis_at] // blocks).reshape([-1 if axis == axis_at else 1 for axis in range(len(dims))])
    return gain


def noise(rng, extent, scale, most, cuts=(), kind=jnp.bfloat16):
    array = jax.random.normal(rng, extent, jnp.float32) * scale
    if len(cuts) > 0:
        array = shard_levels(rng, extent, cuts, -0.22, 0.18) * array
    return jnp.clip(array, min=-most, max=most).astype(kind)


def setup_inputs(seed: int = 0) -> dict:
    key_list = jax.random.split(jax.random.key(seed), 8)
    return {
        "bricks": noise(key_list[0], (N_ROW, N_COL, MAXB, BK, TILE, TILE), (2 * J * K // TILE), 98304.0, ((0, 4), (1, 8))),
        "brick_coords": draw_brick_coords(jax.random.fold_in(key_list[7], 71), 0),
        "brick_counts": draw_brick_counts(jax.random.fold_in(key_list[7], 71), 0),
        "step_sizes": jnp.clip(jnp.exp(jax.random.uniform(key_list[3], (SWEEPS, 3), jnp.float32, math.log(0.3), math.log(1.0))), 0.3, 1.0),
        "init_a": noise(key_list[4], (N_ROW, TI * TILE, R), 1.0, 6.0, ((0, 4), (1, 8)), jnp.float32),
        "init_b": noise(key_list[5], (N_COL, TJ * TILE, R), 1.0, 6.0, ((0, 8), (1, 4)), jnp.float32),
        "init_c": noise(key_list[6], (K, R), 1.0, 6.0, (), jnp.float32),
    }


def brick_terms(brick, a_tile, b_tile, c_rows):
    block = brick.astype(jnp.float32)
    a_full = a_tile.astype(jnp.float32)
    b_full = b_tile.astype(jnp.float32)
    c_wide = c_rows.astype(jnp.float32)[:, None, :]
    wide = jnp.einsum("kij,jr->kir", block, b_full)
    along_a = jnp.sum(wide * c_wide, axis=0)
    deep = jnp.einsum("kij,ir->kjr", block, a_full)
    along_b = jnp.sum(deep * c_wide, axis=0)
    along_c = jnp.sum(deep * b_full[None, :, :], axis=1)
    return along_a, along_b, along_c


def add_tile(total, delta, start):
    old = lax.dynamic_slice_in_dim(total, start, delta.shape[0], 0)
    return lax.dynamic_update_slice_in_dim(total, old + delta, start, 0)


def gram(values):
    return jnp.dot(values.T, values, preferred_element_type=jnp.float32)


def project(state, hess, drive, rate):
    scale = jnp.sum(jnp.abs(hess), axis=1) + 1e-6
    slope = jnp.dot(state, hess, precision=lax.Precision.HIGHEST, preferred_element_type=jnp.float32) - drive
    return jnp.maximum(state - rate * slope / scale[None, :], 0.0)


def reference(bricks, brick_coords, brick_counts, step_sizes, init_a, init_b, init_c):
    slots = N_ROW * N_COL * MAXB
    flat = bricks.reshape(slots, BK, TILE, TILE)
    spots = jnp.transpose(brick_coords, (0, 1, 3, 2)).reshape(slots, 3).astype(jnp.int32)
    number = jnp.arange(slots, dtype=jnp.int32)
    row_of = number // (N_COL * MAXB)
    col_of = (number // MAXB) % N_COL
    slot_of = number % MAXB
    alive = slot_of < brick_counts.reshape(-1)[number // MAXB]
    i_start = ((row_of * TI + spots[:, 0]) * TILE).astype(jnp.int32)
    j_start = ((col_of * TJ + spots[:, 1]) * TILE).astype(jnp.int32)
    k_start = (spots[:, 2] * BK).astype(jnp.int32)
    state_a = init_a.reshape(N_ROW * TI * TILE, R)
    state_b = init_b.reshape(N_COL * TJ * TILE, R)
    state_c = init_c
    for sweep in range(SWEEPS):
        a_bf = state_a.astype(jnp.bfloat16)
        b_bf = state_b.astype(jnp.bfloat16)
        c_bf = state_c.astype(jnp.bfloat16)

        def visit(carry, item):
            brick, live, i_low, j_low, k_low = item

            def work(inner):
                total_a, total_b, total_c = inner
                a_tile = lax.dynamic_slice_in_dim(a_bf, i_low, TILE, 0)
                b_tile = lax.dynamic_slice_in_dim(b_bf, j_low, TILE, 0)
                c_rows = lax.dynamic_slice_in_dim(c_bf, k_low, BK, 0)
                delta_a, delta_b, delta_c = brick_terms(brick, a_tile, b_tile, c_rows)
                return (add_tile(total_a, delta_a, i_low), add_tile(total_b, delta_b, j_low), add_tile(total_c, delta_c, k_low))

            def skip(inner):
                return inner

            return lax.cond(live, work, skip, carry), None

        start = (jnp.zeros(state_a.shape, jnp.float32), jnp.zeros(state_b.shape, jnp.float32), jnp.zeros(state_c.shape, jnp.float32))
        (drive_a, drive_b, drive_c), _ = lax.scan(visit, start, (flat, alive, i_start, j_start, k_start))
        gram_a = gram(a_bf)
        gram_b = gram(b_bf)
        gram_c = gram(c_bf)
        new_a = project(state_a, gram_b * gram_c, drive_a, step_sizes[sweep, 0])
        new_b = project(state_b, gram_a * gram_c, drive_b, step_sizes[sweep, 1])
        new_c = project(state_c, gram_a * gram_b, drive_c, step_sizes[sweep, 2])
        state_a, state_b, state_c = new_a, new_b, new_c
    return state_a.reshape(N_ROW, TI * TILE, R), state_b.reshape(N_COL, TJ * TILE, R), state_c
```

```python
import functools

import jax
import jax.numpy as jnp
from jax import lax
from jax.experimental import pallas as pl
from jax.experimental.pallas import tpu as pltpu
from jax.sharding import PartitionSpec as P

MESH = pl.DeviceIdType.MESH
F32 = jnp.float32
BF16 = jnp.bfloat16


def gram(values):
    return lax.dot_general(
        values, values, (((0,), (0,)), ((), ())), preferred_element_type=F32
    )


def kernel(
    nr, nc, sems_of,
    places, counts, rates, bricks, meta, init_a, init_b, init_c,
    out_a, out_b, out_c,
    flip, a_all, b_all, c_all, acc_a, acc_b,
    da, da1, da_sum, da2, db, db2,
    cc, cpart, c2, csum, c3,
    sa_part, sa1, sa_full, sb_part, sb1, sb2, sb_full,
    send, recv,
):
    nz = nc // 2
    slots, depth, tile, _ = bricks.shape
    rank = init_a.shape[-1]
    ra, rb = init_a.shape[0], init_b.shape[0]
    sweeps = rates.shape[0]
    k_row = init_c.shape[0] // nr
    k_half = k_row // 2
    spots = k_row // depth
    nzc = c_all.shape[3]
    qa, qb = tile // ra, tile // rb
    tiles_i, tiles_j = nc // qa, nr // qb

    r = lax.axis_index("row")
    c = lax.axis_index("col")
    z = lax.div(c, 2)
    core = lax.rem(c, 2)
    other = 1 - core
    used = [0]
    started = []

    def push(src, dst, row, col):
        at = used[0]
        used[0] += 1
        copy = pltpu.make_async_remote_copy(
            src_ref=src, dst_ref=dst, send_sem=send.at[at], recv_sem=recv.at[at],
            device_id=(row, col), device_id_type=MESH,
        )
        copy.start()
        started.append(copy)
        return copy

    def to_core(src, dst):
        return push(src, dst, r, z * 2 + other)

    def row_peer(step):
        return lax.rem(r + step, nr), lax.rem(r + nr - step, nr)

    def z_peer(step):
        return lax.rem(z + step, nz), lax.rem(z + nz - step, nz)

    barrier = pltpu.get_barrier_semaphore()
    pl.semaphore_signal(barrier, inc=1, device_id=(r, z * 2 + other), device_id_type=MESH)
    for step in range(1, nr):
        pl.semaphore_signal(barrier, inc=1, device_id=(row_peer(step)[0], c), device_id_type=MESH)
    for step in range(1, nz):
        pl.semaphore_signal(
            barrier, inc=1, device_id=(r, z_peer(step)[0] * 2 + core), device_id_type=MESH
        )

    live = [counts[0] > slot for slot in range(slots)]
    spot_i = [jnp.clip(places[0, slot], 0, tiles_i - 1) for slot in range(slots)]
    spot_j = [jnp.clip(places[1, slot], 0, tiles_j - 1) for slot in range(slots)]

    def weights(spot, tiles):
        return [
            [
                jnp.where(jnp.logical_and(live[slot], spot[slot] == at), 1.0, 0.0).astype(F32)
                for at in range(tiles)
            ]
            for slot in range(slots)
        ]

    w_i = weights(spot_i, tiles_i)
    w_j = weights(spot_j, tiles_j)

    state_a = init_a[...]
    state_b = init_b[...]
    state_c = init_c[pl.ds(pl.multiple_of(r * k_row + core * k_half, 8), k_half), :]
    if nzc > 1:
        start_c = r * k_row + core * k_half + z * (k_half // nzc)
        state_c = init_c[pl.ds(pl.multiple_of(start_c, 8), k_half // nzc), :]
    c_all[0] = init_c[...].astype(BF16).reshape(c_all.shape[1:])
    a_all[0, c] = state_a.astype(BF16)
    b_all[0, r] = state_b.astype(BF16)

    pl.semaphore_wait(barrier, 1 + (nr - 1) + (nz - 1))

    def send_b(s):
        return [push(b_all.at[s, r], b_all.at[s, r], row_peer(step)[0], c) for step in range(1, nr)]

    def send_a(s):
        near = to_core(a_all.at[s, c], a_all.at[s, c])
        return near, [
            push(a_all.at[s, c], a_all.at[s, c], r, z_peer(step)[0] * 2 + core)
            for step in range(1, nz)
        ]

    def forward_a(s, far):
        passed = []
        for step in range(1, nz):
            far[step - 1].wait_recv()
            at = z_peer(step)[1] * 2 + core
            passed.append(to_core(a_all.at[s, at], a_all.at[s, at]))
        return passed

    def forward_row(ref_at, far):
        passed = [to_core(ref_at(r), ref_at(r))]
        for step in range(1, nr):
            far[step - 1].wait_recv()
            at = row_peer(step)[1]
            passed.append(to_core(ref_at(at), ref_at(at)))
        return passed

    def spread_row(ref_at):
        return [push(ref_at(r), ref_at(r), row_peer(step)[0], c) for step in range(1, nr)]

    def spread_c(ref_at):
        if nzc == 1:
            return []
        return [
            push(ref_at(z), ref_at(z), r, z_peer(step)[0] * 2 + core) for step in range(1, nz)
        ]

    def done(copies):
        for copy in copies:
            copy.wait_recv()

    def total(ref, s, count):
        value = ref[s, 0]
        for at in range(1, count):
            value = value + ref[s, at]
        return value

    far_b = send_b(0)
    near_a, far_a = send_a(0)
    for slot in range(slots):
        def turn(k, carry, slot=slot):
            flip[slot, k] = bricks[slot, k].T
            return carry
        lax.fori_loop(0, depth, turn, 0)
    gram_c = gram(c_all[0].reshape(nr * k_row, rank))
    wait_c = None

    for s in range(sweeps):
        done(far_b)
        sb_part[s] = gram(b_all[s].reshape(nr * rb, rank)).reshape(sb_part.shape[1:])
        step_sb1 = to_core(sb_part.at[s, r, other], sb1.at[s])
        passed_a = forward_a(s, far_a)
        step_sb1.wait_recv()
        sb2[s, z] = sb_part[s, r, core] + sb1[s]
        step_sb2 = [
            push(sb2.at[s, z], sb2.at[s, z], r, z_peer(step)[0] * 2 + core)
            for step in range(1, nz)
        ]
        near_a.wait_recv()
        done(passed_a)
        sa_part[s] = gram(a_all[s].reshape(nc * ra, rank)).reshape(sa_part.shape[1:])
        sa1[s, r] = sa_part[s, core, r]
        step_sa1 = [
            push(sa_part.at[s, core, row_peer(step)[0]], sa1.at[s, r], row_peer(step)[0], c)
            for step in range(1, nr)
        ]
        if wait_c is not None:
            wait_c()

        def tile_b(slot):
            return b_all[s, pl.ds(spot_j[slot] * qb, qb)].reshape(tile, rank)

        def rows_c(slot):
            at = jnp.clip(places[2, slot], 0, nr * spots - 1)
            within = lax.rem(at, spots)
            low = lax.rem(within, spots // 2)
            wide_c = c_all[s, lax.div(at, spots), lax.div(within, spots // 2)]
            picked = jnp.zeros((depth, rank), F32)
            flat = wide_c.astype(F32).reshape(spots // 2, depth, rank)
            for one in range(spots // 2):
                picked = picked + flat[one] * jnp.where(low == one, 1.0, 0.0).astype(F32)
            return picked

        c_rows = [rows_c(slot) for slot in range(slots)]
        for slot in range(slots):
            b_tile = tile_b(slot)
            sums = jnp.zeros((tile, rank), F32)
            for k in range(depth):
                wide = jnp.dot(bricks[slot, k], b_tile, preferred_element_type=F32)
                sums = sums + wide * c_rows[slot][k:k + 1]
            acc_a[slot] = sums
        for g in range(nc):
            at, off = g // qa, (g % qa) * ra
            da[s, g % 2, g // 2] = sum(
                w_i[slot][at] * acc_a[slot, off:off + ra, :] for slot in range(slots)
            )
        step_da1 = {}
        for step in list(range(1, nz)) + [0]:
            to = z_peer(step)[0]
            step_da1[step] = to_core(da.at[s, other, to], da1.at[s, to])

        done(step_sa1)
        sa_full[s, core, r] = total(sa1, s, nr)
        step_sa2 = spread_row(lambda at: sa_full.at[s, core, at])

        for slot in range(slots):
            a_tile = a_all[s, pl.ds(spot_i[slot] * qa, qa)].reshape(tile, rank)
            b_tile = tile_b(slot).astype(F32)
            sums = jnp.zeros((tile, rank), F32)
            along_c = []
            for k in range(depth):
                deep = jnp.dot(flip[slot, k], a_tile, preferred_element_type=F32)
                sums = sums + deep * c_rows[slot][k:k + 1]
                along_c.append(jnp.sum(deep * b_tile, axis=0, keepdims=True))
            acc_b[slot] = sums
            cc[s, r, slot * depth:(slot + 1) * depth, :] = jnp.concatenate(along_c, axis=0)
        cc[s, r, slots * depth:, :] = meta[...]
        step_c1 = spread_row(lambda at: cc.at[s, at])
        for g in range(nr):
            at, off = g // qb, (g % qb) * rb
            db[s, g] = sum(
                w_j[slot][at] * acc_b[slot, off:off + rb, :] for slot in range(slots)
            )
        db2[s, r] = db[s, r]
        step_db = [
            push(db.at[s, row_peer(step)[0]], db2.at[s, r], row_peer(step)[0], c)
            for step in range(1, nr)
        ]

        step_da2 = []
        for step in list(range(1, nz)) + [0]:
            to = z_peer(step)[0]
            step_da1[step].wait_recv()
            if step == 0:
                da2[s, z] = da[s, core, z] + da1[s, z]
            else:
                da_sum[s, to] = da[s, core, to] + da1[s, to]
                step_da2.append(push(da_sum.at[s, to], da2.at[s, z], r, to * 2 + core))

        done(step_sb2)
        sb_full[s, r, core] = total(sb2, s, nz)
        step_sb3 = spread_row(lambda at: sb_full.at[s, at, core])
        step_sa3 = forward_row(lambda at: sa_full.at[s, core, at], step_sa2)

        done(step_c1)
        for one in range(spots):
            want = (r * spots + one).astype(F32)
            sums = jnp.zeros((depth, rank), F32)
            for src in range(nr):
                for slot in range(slots):
                    tag = cc[s, src, slots * depth + slot:slots * depth + slot + 1, :]
                    term = cc[s, src, slot * depth:(slot + 1) * depth, :]
                    sums = sums + jnp.where(tag == want, term, 0.0)
            half = spots // 2
            cpart[s, one // half, (one % half) * depth:(one % half + 1) * depth, :] = sums
        step_c2 = to_core(cpart.at[s, other], c2.at[s])
        step_sb4 = forward_row(lambda at: sb_full.at[s, at, core], step_sb3)
        step_c2.wait_recv()
        csum[s] = (cpart[s, core] + c2[s]).reshape(csum.shape[1:])
        mine = z if nzc > 1 else 0
        c3[s, z] = csum[s, mine]
        step_c3 = []
        for step in range(1, nz):
            to = z_peer(step)[0]
            step_c3.append(
                push(csum.at[s, to if nzc > 1 else 0], c3.at[s, z], r, to * 2 + core)
            )

        def prepare(state, hess):
            scale = jnp.sum(jnp.abs(hess), axis=0, keepdims=True) + 1e-06
            moved = jnp.dot(
                state, hess, precision=lax.Precision.HIGHEST, preferred_element_type=F32
            )
            return moved, scale

        def finish(state, ready, drive, rate):
            moved, scale = ready
            return jnp.maximum(state - rate * (moved - drive) / scale, 0.0)

        last = s == sweeps - 1
        done(step_sa3)
        gram_a = sa_full[s].reshape(rank, rank)
        ready_b = prepare(state_b, gram_a * gram_c)
        done(step_db)
        state_b = finish(state_b, ready_b, total(db2, s, nr), rates[s, 1])
        if last:
            out_b[...] = state_b
        else:
            b_all[s + 1, r] = state_b.astype(BF16)
            far_b = send_b(s + 1)
        done(step_sb4)
        gram_b = sb_full[s].reshape(rank, rank)
        ready_c = prepare(state_c, gram_a * gram_b)
        done(step_c3)
        state_c = finish(state_c, ready_c, total(c3, s, nz), rates[s, 2])
        if last:
            part = lambda at: out_c.at[r, core, at]
            rows = lambda at: out_c.at[at, core]
            out_c[r, core, mine] = state_c
        else:
            part = lambda at, s=s: c_all.at[s + 1, r, core, at]
            rows = lambda at, s=s: c_all.at[s + 1, at, core]
            c_all[s + 1, r, core, mine] = state_c.astype(BF16)
        far_c = spread_c(part)
        ready_a = prepare(state_a, gram_b * gram_c)
        done(step_da2)
        state_a = finish(state_a, ready_a, total(da2, s, nz), rates[s, 0])
        if last:
            out_a[...] = state_a
        else:
            a_all[s + 1, c] = state_a.astype(BF16)
            near_a, far_a = send_a(s + 1)
        done(far_c)
        far_c = spread_row(rows)
        if last:
            done(forward_row(rows, far_c))
        else:
            passed_c = forward_row(rows, far_c)
            done(passed_c)
            gram_c = gram(c_all[s + 1].reshape(nr * k_row, rank))

    for copy in started:
        copy.wait_send()
    assert used[0] <= sems_of


def shards(nr, nc, bricks, brick_coords, brick_counts, step_sizes, init_a, init_b, init_c):
    slab = bricks[0, 0]
    places = brick_coords[0, 0]
    counts = brick_counts[0]
    slots, depth, tile, _ = slab.shape
    sweeps = step_sizes.shape[0]
    ra, rank = init_a.shape[1:]
    rb = init_b.shape[1]
    depth_c = init_c.shape[0]
    nz = nc // 2
    k_row = depth_c // nr
    k_half = k_row // 2
    nzc = nz if k_half % (nz * 16) == 0 else 1
    rc = k_half // nzc
    tags = -(-slots // 8) * 8
    alive = jnp.arange(slots) < counts[0]
    tag = jnp.where(alive, places[2], -1).astype(F32)
    meta = jnp.broadcast_to(jnp.pad(tag, (0, tags - slots))[:, None], (tags, rank))
    sems = sweeps * (2 * nz + 1 + (nr - 1) + 2 + nz + 4 * nr + nz + nz + 2 * nr + nr + 1 + nz + nz + 6 * nr)
    vmem = pl.BlockSpec(memory_space=pltpu.VMEM)
    smem = pl.BlockSpec(memory_space=pltpu.SMEM)
    scratch = [
        ((slots, depth, tile, tile), BF16),
        ((sweeps, nc, ra, rank), BF16),
        ((sweeps, nr, rb, rank), BF16),
        ((sweeps, nr, 2, nzc, rc, rank), BF16),
        ((slots, tile, rank), F32),
        ((slots, tile, rank), F32),
        ((sweeps, 2, nz, ra, rank), F32),
        ((sweeps, nz, ra, rank), F32),
        ((sweeps, nz, ra, rank), F32),
        ((sweeps, nz, ra, rank), F32),
        ((sweeps, nr, rb, rank), F32),
        ((sweeps, nr, rb, rank), F32),
        ((sweeps, nr, slots * depth + tags, rank), F32),
        ((sweeps, 2, k_half, rank), F32),
        ((sweeps, k_half, rank), F32),
        ((sweeps, nzc, rc, rank), F32),
        ((sweeps, nz, rc, rank), F32),
        ((sweeps, 2, nr, rank // nr // 2, rank), F32),
        ((sweeps, nr, rank // nr // 2, rank), F32),
        ((sweeps, 2, nr, rank // nr // 2, rank), F32),
        ((sweeps, nr, 2, rank // nr // 2, rank), F32),
        ((sweeps, rank // nr // 2, rank), F32),
        ((sweeps, nz, rank // nr // 2, rank), F32),
        ((sweeps, nr, 2, rank // nr // 2, rank), F32),
    ]
    new_a, new_b, new_c = pl.pallas_call(
        functools.partial(kernel, nr, nc, sems),
        out_shape=(
            jax.ShapeDtypeStruct((ra, rank), F32),
            jax.ShapeDtypeStruct((rb, rank), F32),
            jax.ShapeDtypeStruct((nr, 2, nzc, rc, rank), F32),
        ),
        in_specs=[smem, smem, smem] + [vmem] * 5,
        out_specs=(vmem, vmem, vmem),
        scratch_shapes=[pltpu.VMEM(*one) for one in scratch]
        + [pltpu.SemaphoreType.DMA((sems,)), pltpu.SemaphoreType.DMA((sems,))],
        compiler_params=pltpu.CompilerParams(
            collective_id=0, has_side_effects=True, vmem_limit_bytes=48 * 1024 * 1024
        ),
        name="sweeps",
    )(places, counts, step_sizes, slab, meta, init_a[0], init_b[0], init_c)
    return new_a[None], new_b[None], new_c.reshape(depth_c, rank)


def solution(mesh):
    placed = (
        P("row", "col", None, None, None, None),
        P("row", "col", None, None),
        P("row", "col"),
        P(),
        P("row", "col", None),
        P("col", "row", None),
        P(),
    )
    return jax.shard_map(
        functools.partial(shards, mesh.shape["row"], mesh.shape["col"]),
        mesh=mesh,
        in_specs=placed,
        out_specs=(P("row", "col", None), P("col", "row", None), P()),
        check_vma=False,
    )
```

```python
import functools

import jax
import jax.numpy as jnp
from jax import lax
from jax.experimental import pallas as pl
from jax.experimental.pallas import tpu as pltpu
from jax.sharding import PartitionSpec as P

MESH = pl.DeviceIdType.MESH
F32 = jnp.float32
BF16 = jnp.bfloat16


def gram(values):
    return lax.dot_general(
        values, values, (((0,), (0,)), ((), ())), preferred_element_type=F32
    )


def kernel(
    nr, nc, sems_of,
    places, counts, rates, far_bricks, far_a0, far_b0, far_c0,
    out_a, out_b, out_c,
    bricks, init_a, init_b, init_c,
    flip, a_all, b_all, c_all, acc_a, acc_b, spread,
    da, da1, da_sum, da2, db, db2,
    cc, tags, csum, c3,
    sa_part, sa1, sa_full, sb_part, sb1, sb2, sb_full,
    load, send, recv,
):
    nz = nc // 2
    slots, depth, tile, _ = bricks.shape
    rank = init_a.shape[-1]
    ra, rb = init_a.shape[0], init_b.shape[0]
    sweeps = rates.shape[0]
    k_row = init_c.shape[0] // nr
    k_half = k_row // 2
    spots = k_row // depth
    nzc = c_all[0].shape[2]
    qa, qb = tile // ra, tile // rb
    tiles_i, tiles_j = nc // qa, nr // qb

    loads = [
        pltpu.make_async_copy(src, dst, load.at[at])
        for at, (src, dst) in enumerate(
            ((far_b0, init_b), (far_a0, init_a), (far_c0, init_c), (far_bricks, bricks))
        )
    ]
    for copy in loads:
        copy.start()

    r = lax.axis_index("row")
    c = lax.axis_index("col")
    z = lax.div(c, 2)
    core = lax.rem(c, 2)
    other = 1 - core
    used = [0]
    started = []

    def push(src, dst, row, col):
        at = used[0]
        used[0] += 1
        copy = pltpu.make_async_remote_copy(
            src_ref=src, dst_ref=dst, send_sem=send.at[at], recv_sem=recv.at[at],
            device_id=(row, col), device_id_type=MESH,
        )
        copy.start()
        started.append(copy)
        return copy

    def to_core(src, dst):
        return push(src, dst, r, z * 2 + other)

    def row_peer(step):
        return lax.rem(r + step, nr), lax.rem(r + nr - step, nr)

    def z_peer(step):
        return lax.rem(z + step, nz), lax.rem(z + nz - step, nz)

    barrier = pltpu.get_barrier_semaphore()
    pl.semaphore_signal(barrier, inc=1, device_id=(r, z * 2 + other), device_id_type=MESH)
    for step in range(1, nr):
        for col in (c, z * 2 + other):
            pl.semaphore_signal(
                barrier, inc=1, device_id=(row_peer(step)[0], col), device_id_type=MESH
            )
    for step in range(1, nz):
        pl.semaphore_signal(
            barrier, inc=1, device_id=(r, z_peer(step)[0] * 2 + core), device_id_type=MESH
        )

    live = [counts[0, 0] > slot for slot in range(slots)]
    spot_i = [jnp.clip(places[0, 0, slot, 0], 0, tiles_i - 1) for slot in range(slots)]
    spot_j = [jnp.clip(places[0, 0, slot, 1], 0, tiles_j - 1) for slot in range(slots)]

    def weights(spot, tiles):
        return [
            [
                jnp.where(jnp.logical_and(live[slot], spot[slot] == at), 1.0, 0.0).astype(F32)
                for at in range(tiles)
            ]
            for slot in range(slots)
        ]

    w_i = weights(spot_i, tiles_i)
    w_j = weights(spot_j, tiles_j)

    spot_k = [jnp.clip(places[0, 0, slot, 2], 0, nr * spots - 1) for slot in range(slots)]
    number = lax.broadcasted_iota(jnp.int32, tags.shape[2:], 0)
    tag = jnp.full(tags.shape[2:], -1.0, F32)
    for slot in range(slots):
        mark = jnp.where(live[slot], spot_k[slot], -1).astype(F32)
        tag = jnp.where(number == slot, mark, tag)
    tags[r, core] = tag

    loads[0].wait()
    state_b = init_b[...]
    b_all[0][r] = state_b.astype(BF16)
    loads[1].wait()
    state_a = init_a[...]
    a_all[0][c] = state_a.astype(BF16)

    pl.semaphore_wait(barrier, 1 + 2 * (nr - 1) + (nz - 1))

    def send_b(s):
        return [push(b_all[s].at[r], b_all[s].at[r], row_peer(step)[0], c) for step in range(1, nr)]

    def send_a(s):
        near = to_core(a_all[s].at[c], a_all[s].at[c])
        return near, [
            push(a_all[s].at[c], a_all[s].at[c], r, z_peer(step)[0] * 2 + core)
            for step in range(1, nz)
        ]

    def forward_a(s, far):
        passed = []
        for step in range(1, nz):
            far[step - 1].wait_recv()
            at = z_peer(step)[1] * 2 + core
            passed.append(to_core(a_all[s].at[at], a_all[s].at[at]))
        return passed

    def forward_row(ref_at, far):
        passed = [to_core(ref_at(r), ref_at(r))]
        for step in range(1, nr):
            far[step - 1].wait_recv()
            at = row_peer(step)[1]
            passed.append(to_core(ref_at(at), ref_at(at)))
        return passed

    def spread_row(ref_at):
        return [push(ref_at(r), ref_at(r), row_peer(step)[0], c) for step in range(1, nr)]

    def spread_chips(ref):
        copies = [to_core(ref, ref)]
        for step in range(1, nr):
            for col in (c, z * 2 + other):
                copies.append(push(ref, ref, row_peer(step)[0], col))
        return copies

    def spread_c(ref_at):
        if nzc == 1:
            return []
        return [
            push(ref_at(z), ref_at(z), r, z_peer(step)[0] * 2 + core) for step in range(1, nz)
        ]

    def done(copies):
        for copy in copies:
            copy.wait_recv()

    def total(ref, s, count):
        value = ref[s, 0]
        for at in range(1, count):
            value = value + ref[s, at]
        return value

    def turn(slot):
        def one(k, carry):
            flip[slot, k] = bricks[slot, k].T
            return carry
        lax.fori_loop(0, depth, one, 0, unroll=4)

    def tile_a(s, slot):
        return a_all[s][pl.ds(spot_i[slot] * qa, qa)].reshape(tile, rank)

    def tile_b(s, slot):
        return b_all[s][pl.ds(spot_j[slot] * qb, qb)].reshape(tile, rank)

    def rows_c(s, slot):
        at = spot_k[slot]
        within = lax.rem(at, spots)
        low = lax.rem(within, spots // 2)
        wide_c = c_all[s][lax.div(at, spots), lax.div(within, spots // 2)]
        flat = wide_c.astype(F32).reshape(spots // 2, depth, rank)
        picked = jnp.zeros((depth, rank), F32)
        for one in range(spots // 2):
            picked = picked + flat[one] * jnp.where(low == one, 1.0, 0.0).astype(F32)
        return picked

    strip = 8
    batch = 4

    def fill(value_at, right):
        for k in range(0, depth, batch):
            spread[k * tile:(k + batch) * tile, :] = jnp.dot(
                value_at(k).reshape(batch * tile, tile), right, preferred_element_type=F32
            )

    def wide_pass(s, slot):
        fill(lambda k: bricks[slot, k:k + batch], tile_b(s, slot))
        c_rows = rows_c(s, slot)
        acc_b[slot] = tile_a(s, slot).astype(F32)

        def body(at, carry):
            low = pl.multiple_of(at * strip, strip)
            a_rows = acc_b[slot, pl.ds(low, strip), :]
            sums = jnp.zeros((strip, rank), F32)
            along_c = []
            for k in range(depth):
                part = spread[pl.ds(pl.multiple_of(k * tile + low, strip), strip), :]
                sums = sums + part * c_rows[k:k + 1]
                along_c.append(carry[k] + part * a_rows)
            acc_a[slot, pl.ds(low, strip), :] = sums
            return tuple(along_c)

        empty = tuple(jnp.zeros((strip, rank), F32) for _ in range(depth))
        along_c = lax.fori_loop(0, tile // strip, body, empty)
        cc[s, r, core, slot * depth:(slot + 1) * depth, :] = jnp.concatenate(
            [jnp.sum(one, axis=0, keepdims=True) for one in along_c], axis=0
        )

    def deep_pass(s, slot):
        fill(lambda k: flip[slot, k:k + batch], tile_a(s, slot))
        c_rows = rows_c(s, slot)

        def body(at, carry):
            low = pl.multiple_of(at * strip, strip)
            sums = jnp.zeros((strip, rank), F32)
            for k in range(depth):
                part = spread[pl.ds(pl.multiple_of(k * tile + low, strip), strip), :]
                sums = sums + part * c_rows[k:k + 1]
            acc_b[slot, pl.ds(low, strip), :] = sums
            return carry

        lax.fori_loop(0, tile // strip, body, 0)

    far_b = send_b(0)
    near_a, far_a = send_a(0)
    far_tags = spread_chips(tags.at[r, core])
    loads[2].wait()
    mine = z if nzc > 1 else 0
    start_c = r * k_row + core * k_half + mine * (k_half // nzc)
    state_c = init_c[pl.ds(pl.multiple_of(start_c, 8), k_half // nzc), :]
    c_all[0][...] = init_c[...].astype(BF16).reshape(c_all[0].shape)
    gram_c = gram(c_all[0][...].reshape(nr * k_row, rank))
    loads[3].wait()
    wait_c = []

    for s in range(sweeps):
        done(far_b)
        sb_part[s] = gram(b_all[s][...].reshape(nr * rb, rank)).reshape(sb_part.shape[1:])
        step_sb1 = to_core(sb_part.at[s, r, other], sb1.at[s])
        passed_a = forward_a(s, far_a)
        step_sb1.wait_recv()
        sb2[s, z] = sb_part[s, r, core] + sb1[s]
        step_sb2 = [
            push(sb2.at[s, z], sb2.at[s, z], r, z_peer(step)[0] * 2 + core)
            for step in range(1, nz)
        ]
        near_a.wait_recv()
        done(passed_a)
        sa_part[s] = gram(a_all[s][...].reshape(nc * ra, rank)).reshape(sa_part.shape[1:])
        sa1[s, r] = sa_part[s, core, r]
        step_sa1 = [
            push(sa_part.at[s, core, row_peer(step)[0]], sa1.at[s, r], row_peer(step)[0], c)
            for step in range(1, nr)
        ]
        done(wait_c)
        for slot in range(slots):
            wide_pass(s, slot)
        step_c1 = spread_chips(cc.at[s, r, core])
        for g in range(nc):
            at, off = g // qa, (g % qa) * ra
            da[s, g % 2, g // 2] = sum(
                w_i[slot][at] * acc_a[slot, off:off + ra, :] for slot in range(slots)
            )
        step_da1 = {}
        for step in list(range(1, nz)) + [0]:
            to = z_peer(step)[0]
            step_da1[step] = to_core(da.at[s, other, to], da1.at[s, to])

        done(step_sa1)
        sa_full[s, core, r] = total(sa1, s, nr)
        step_sa2 = spread_row(lambda at: sa_full.at[s, core, at])
        done(step_sb2)
        sb_full[s, r, core] = total(sb2, s, nz)
        step_sb3 = spread_row(lambda at: sb_full.at[s, at, core])

        step_da2 = []
        for step in list(range(1, nz)) + [0]:
            to = z_peer(step)[0]
            step_da1[step].wait_recv()
            if step == 0:
                da2[s, z] = da[s, core, z] + da1[s, z]
            else:
                da_sum[s, to] = da[s, core, to] + da1[s, to]
                step_da2.append(push(da_sum.at[s, to], da2.at[s, z], r, to * 2 + core))

        done(step_c1)
        if s == 0:
            done(far_tags)
        half = spots // 2
        found = []
        for one in range(half):
            want = (r * spots + core * half + one).astype(F32)
            sums = jnp.zeros((depth, rank), F32)
            for src in range(nr):
                for side in range(2):
                    for slot in range(slots):
                        term = cc[s, src, side, slot * depth:(slot + 1) * depth, :]
                        mark = tags[src, side, slot:slot + 1, :]
                        sums = sums + jnp.where(mark == want, term, 0.0)
            found.append(sums)
        csum[s] = jnp.concatenate(found, axis=0).reshape(csum.shape[1:])
        c3[s, z] = csum[s, mine]
        step_c3 = []
        for step in range(1, nz):
            to = z_peer(step)[0]
            step_c3.append(
                push(csum.at[s, to if nzc > 1 else 0], c3.at[s, z], r, to * 2 + core)
            )

        for slot in range(slots):
            if s == 0:
                turn(slot)
            deep_pass(s, slot)
        for g in range(nr):
            at, off = g // qb, (g % qb) * rb
            db[s, g] = sum(
                w_j[slot][at] * acc_b[slot, off:off + rb, :] for slot in range(slots)
            )
        db2[s, r] = db[s, r]
        step_db = [
            push(db.at[s, row_peer(step)[0]], db2.at[s, r], row_peer(step)[0], c)
            for step in range(1, nr)
        ]

        step_sa3 = forward_row(lambda at: sa_full.at[s, core, at], step_sa2)
        step_sb4 = forward_row(lambda at: sb_full.at[s, at, core], step_sb3)

        def prepare(state, hess):
            scale = jnp.sum(jnp.abs(hess), axis=0, keepdims=True) + 1e-06
            high = hess.astype(BF16)
            low = (hess - high.astype(F32)).astype(BF16)
            top = state.astype(BF16)
            rest = (state - top.astype(F32)).astype(BF16)
            rows = state.shape[0]
            both = jnp.dot(
                jnp.concatenate([top, rest], axis=0), high, preferred_element_type=F32
            )
            moved = both[:rows] + both[rows:] + jnp.dot(top, low, preferred_element_type=F32)
            return moved, scale

        def finish(state, ready, drive, rate):
            moved, scale = ready
            return jnp.maximum(state - rate * (moved - drive) / scale, 0.0)

        last = s == sweeps - 1
        done(step_sa3)
        gram_a = sa_full[s].reshape(rank, rank)
        done(step_sb4)
        gram_b = sb_full[s].reshape(rank, rank)
        ready_c = prepare(state_c, gram_a * gram_b)
        done(step_c3)
        state_c = finish(state_c, ready_c, total(c3, s, nz), rates[s, 2])
        if last:
            out_c[r, core, mine] = state_c
            far_c = spread_c(lambda at: out_c.at[r, core, at])
        else:
            c_all[s + 1][r, core, mine] = state_c.astype(BF16)
            far_c = spread_c(lambda at: c_all[s + 1].at[r, core, at])
        ready_b = prepare(state_b, gram_a * gram_c)
        done(step_db)
        state_b = finish(state_b, ready_b, total(db2, s, nr), rates[s, 1])
        if last:
            out_b[...] = state_b
        else:
            b_all[s + 1][r] = state_b.astype(BF16)
            far_b = send_b(s + 1)
        done(far_c)
        if last:
            far_c = spread_row(lambda at: out_c.at[at, core])
        else:
            wait_c = spread_chips(c_all[s + 1].at[r, core])
        ready_a = prepare(state_a, gram_b * gram_c)
        done(step_da2)
        state_a = finish(state_a, ready_a, total(da2, s, nz), rates[s, 0])
        if last:
            out_a[...] = state_a
            done(forward_row(lambda at: out_c.at[at, core], far_c))
        else:
            a_all[s + 1][c] = state_a.astype(BF16)
            near_a, far_a = send_a(s + 1)
            done(wait_c)
            wait_c = []
            gram_c = gram(c_all[s + 1][...].reshape(nr * k_row, rank))

    for copy in started:
        copy.wait_send()
    assert used[0] <= sems_of


def shards(nr, nc, bricks, brick_coords, brick_counts, step_sizes, init_a, init_b, init_c):
    slots, depth, tile, _ = bricks.shape[2:]
    sweeps = step_sizes.shape[0]
    ra, rank = init_a.shape[1:]
    rb = init_b.shape[1]
    depth_c = init_c.shape[0]
    nz = nc // 2
    k_row = depth_c // nr
    k_half = k_row // 2
    nzc = nz if k_half % (nz * 16) == 0 else 1
    rc = k_half // nzc
    tags = -(-slots // 8) * 8
    sems = 2 * nr + sweeps * (6 * nz + 13 * nr)
    vmem = pl.BlockSpec(memory_space=pltpu.VMEM)
    smem = pl.BlockSpec(memory_space=pltpu.SMEM)
    far = pl.BlockSpec(memory_space=pltpu.HBM)
    scratch = [
        ((slots, depth, tile, tile), BF16),
        ((ra, rank), F32),
        ((rb, rank), F32),
        ((depth_c, rank), F32),
        ((slots, depth, tile, tile), BF16),
        [((nc, ra, rank), BF16)] * sweeps,
        [((nr, rb, rank), BF16)] * sweeps,
        [((nr, 2, nzc, rc, rank), BF16)] * sweeps,
        ((slots, tile, rank), F32),
        ((slots, tile, rank), F32),
        ((depth * tile, rank), F32),
        ((sweeps, 2, nz, ra, rank), F32),
        ((sweeps, nz, ra, rank), F32),
        ((sweeps, nz, ra, rank), F32),
        ((sweeps, nz, ra, rank), F32),
        ((sweeps, nr, rb, rank), F32),
        ((sweeps, nr, rb, rank), F32),
        ((sweeps, nr, 2, slots * depth, rank), F32),
        ((nr, 2, tags, rank), F32),
        ((sweeps, nzc, rc, rank), F32),
        ((sweeps, nz, rc, rank), F32),
        ((sweeps, 2, nr, rank // nr // 2, rank), F32),
        ((sweeps, nr, rank // nr // 2, rank), F32),
        ((sweeps, 2, nr, rank // nr // 2, rank), F32),
        ((sweeps, nr, 2, rank // nr // 2, rank), F32),
        ((sweeps, rank // nr // 2, rank), F32),
        ((sweeps, nz, rank // nr // 2, rank), F32),
        ((sweeps, nr, 2, rank // nr // 2, rank), F32),
    ]
    new_a, new_b, new_c = pl.pallas_call(
        functools.partial(kernel, nr, nc, sems),
        out_shape=(
            jax.ShapeDtypeStruct((ra, rank), F32),
            jax.ShapeDtypeStruct((rb, rank), F32),
            jax.ShapeDtypeStruct((nr, 2, nzc, rc, rank), F32),
        ),
        in_specs=[smem, smem, smem] + [far] * 4,
        out_specs=(vmem, vmem, vmem),
        scratch_shapes=[
            [pltpu.VMEM(*each) for each in one] if isinstance(one, list) else pltpu.VMEM(*one)
            for one in scratch
        ]
        + [pltpu.SemaphoreType.DMA((4,)), pltpu.SemaphoreType.DMA((sems,)), pltpu.SemaphoreType.DMA((sems,))],
        compiler_params=pltpu.CompilerParams(
            collective_id=0, has_side_effects=True, vmem_limit_bytes=64 * 1024 * 1024 - 256 * 1024
        ),
        name="sweeps",
    )(
        jnp.swapaxes(brick_coords, 2, 3), brick_counts, step_sizes,
        bricks.reshape(slots, depth, tile, tile), init_a[0], init_b[0], init_c,
    )
    return new_a[None], new_b[None], new_c.reshape(depth_c, rank)


def solution(mesh):
    placed = (
        P("row", "col", None, None, None, None),
        P("row", "col", None, None),
        P("row", "col"),
        P(),
        P("row", "col", None),
        P("col", "row", None),
        P(),
    )
    return jax.shard_map(
        functools.partial(shards, mesh.shape["row"], mesh.shape["col"]),
        mesh=mesh,
        in_specs=placed,
        out_specs=(P("row", "col", None), P("col", "row", None), P()),
        check_vma=False,
    )
```

```python
import functools

import jax
import jax.numpy as jnp
from jax import lax
from jax.experimental import pallas as pl
from jax.experimental.pallas import tpu as pltpu
from jax.sharding import PartitionSpec as P

MESH = pl.DeviceIdType.MESH
F32 = jnp.float32
BF16 = jnp.bfloat16
VMEM_BYTES = 64 * 1024 * 1024 - 256 * 1024


def gram(values):
    return lax.dot_general(
        values, values, (((0,), (0,)), ((), ())), preferred_element_type=F32
    )


def kernel(
    nr, nc, sems_of,
    places, counts, rates, far_bricks, far_a0, far_b0, far_c0,
    out_a, out_b, out_c,
    bricks, init_a, init_b, init_c,
    flip, a_all, b_all, c_all, acc_a, acc_b, spread, deep_all, final_c,
    da, da1, da_sum, da2, db, db2,
    cc, tags, csum, c3,
    sa_part, sa1, sa_full, sb_part, sb1, sb2, sb_full,
    load, store, send, recv,
):
    nz = nc // 2
    slots, depth, tile, _ = bricks.shape
    rank = init_a.shape[-1]
    ra, rb = init_a.shape[0], init_b.shape[0]
    sweeps = rates.shape[0]
    k_row = init_c.shape[0] // nr
    k_half = k_row // 2
    spots = k_row // depth
    nzc = c_all[0].shape[2]
    qa, qb = tile // ra, tile // rb
    tiles_i, tiles_j = nc // qa, nr // qb

    loads = [
        pltpu.make_async_copy(src, dst, load.at[at])
        for at, (src, dst) in enumerate(
            ((far_b0, init_b), (far_a0, init_a), (far_c0, init_c), (far_bricks, bricks))
        )
    ]
    for copy in loads:
        copy.start()

    r = lax.axis_index("row")
    c = lax.axis_index("col")
    z = lax.div(c, 2)
    core = lax.rem(c, 2)
    other = 1 - core
    used = [0]
    started = []

    def push(src, dst, row, col):
        at = used[0]
        used[0] += 1
        copy = pltpu.make_async_remote_copy(
            src_ref=src, dst_ref=dst, send_sem=send.at[at], recv_sem=recv.at[at],
            device_id=(row, col), device_id_type=MESH,
        )
        copy.start()
        started.append(copy)
        return copy

    def to_core(src, dst):
        return push(src, dst, r, z * 2 + other)

    def row_peer(step):
        return lax.rem(r + step, nr), lax.rem(r + nr - step, nr)

    def z_peer(step):
        return lax.rem(z + step, nz), lax.rem(z + nz - step, nz)

    barrier = pltpu.get_barrier_semaphore()
    pl.semaphore_signal(barrier, inc=1, device_id=(r, z * 2 + other), device_id_type=MESH)
    for step in range(1, nr):
        for col in (c, z * 2 + other):
            pl.semaphore_signal(
                barrier, inc=1, device_id=(row_peer(step)[0], col), device_id_type=MESH
            )
    for step in range(1, nz):
        pl.semaphore_signal(
            barrier, inc=1, device_id=(r, z_peer(step)[0] * 2 + core), device_id_type=MESH
        )

    live = [counts[0, 0] > slot for slot in range(slots)]
    spot_i = [jnp.clip(places[0, 0, slot, 0], 0, tiles_i - 1) for slot in range(slots)]
    spot_j = [jnp.clip(places[0, 0, slot, 1], 0, tiles_j - 1) for slot in range(slots)]

    def weights(spot, tiles):
        return [
            [
                jnp.where(jnp.logical_and(live[slot], spot[slot] == at), 1.0, 0.0).astype(F32)
                for at in range(tiles)
            ]
            for slot in range(slots)
        ]

    w_i = weights(spot_i, tiles_i)
    w_j = weights(spot_j, tiles_j)

    spot_k = [jnp.clip(places[0, 0, slot, 2], 0, nr * spots - 1) for slot in range(slots)]
    number = lax.broadcasted_iota(jnp.int32, tags.shape[2:], 0)
    tag = jnp.full(tags.shape[2:], -1.0, F32)
    for slot in range(slots):
        mark = jnp.where(live[slot], spot_k[slot], -1).astype(F32)
        tag = jnp.where(number == slot, mark, tag)
    tags[r, core] = tag

    loads[0].wait()
    state_b = init_b[...]
    b_all[0][r] = state_b.astype(BF16)
    loads[1].wait()
    state_a = init_a[...]
    a_all[0][c] = state_a.astype(BF16)

    pl.semaphore_wait(barrier, 1 + 2 * (nr - 1) + (nz - 1))

    def send_b(s):
        return [push(b_all[s].at[r], b_all[s].at[r], row_peer(step)[0], c) for step in range(1, nr)]

    def send_a(s):
        near = to_core(a_all[s].at[c], a_all[s].at[c])
        return near, [
            push(a_all[s].at[c], a_all[s].at[c], r, z_peer(step)[0] * 2 + core)
            for step in range(1, nz)
        ]

    def forward_a(s, far):
        passed = []
        for step in range(1, nz):
            far[step - 1].wait_recv()
            at = z_peer(step)[1] * 2 + core
            passed.append(to_core(a_all[s].at[at], a_all[s].at[at]))
        return passed

    def forward_row(ref_at, far):
        passed = [to_core(ref_at(r), ref_at(r))]
        for step in range(1, nr):
            far[step - 1].wait_recv()
            at = row_peer(step)[1]
            passed.append(to_core(ref_at(at), ref_at(at)))
        return passed

    def spread_row(ref_at):
        return [push(ref_at(r), ref_at(r), row_peer(step)[0], c) for step in range(1, nr)]

    def spread_chips(ref):
        copies = [to_core(ref, ref)]
        for step in range(1, nr):
            for col in (c, z * 2 + other):
                copies.append(push(ref, ref, row_peer(step)[0], col))
        return copies

    def spread_c(ref_at):
        if nzc == 1:
            return []
        return [
            push(ref_at(z), ref_at(z), r, z_peer(step)[0] * 2 + core) for step in range(1, nz)
        ]

    def done(copies):
        for copy in copies:
            copy.wait_recv()

    def total(ref, s, count):
        value = ref[s, 0]
        for at in range(1, count):
            value = value + ref[s, at]
        return value

    def turn(slot):
        def one(k, carry):
            flip[slot, k] = bricks[slot, k].T
            return carry
        lax.fori_loop(0, depth, one, 0, unroll=4)

    def tile_a(s, slot):
        return a_all[s][pl.ds(spot_i[slot] * qa, qa)].reshape(tile, rank)

    def tile_b(s, slot):
        return b_all[s][pl.ds(spot_j[slot] * qb, qb)].reshape(tile, rank)

    def rows_c(s, slot):
        at = spot_k[slot]
        within = lax.rem(at, spots)
        low = lax.rem(within, spots // 2)
        wide_c = c_all[s][lax.div(at, spots), lax.div(within, spots // 2)]
        flat = wide_c.astype(F32).reshape(spots // 2, depth, rank)
        picked = jnp.zeros((depth, rank), F32)
        for one in range(spots // 2):
            picked = picked + flat[one] * jnp.where(low == one, 1.0, 0.0).astype(F32)
        return picked

    strip = 8
    batch = 4

    def fill(wide, value_at, right):
        for k in range(0, depth, batch):
            wide[k * tile:(k + batch) * tile, :] = jnp.dot(
                value_at(k).reshape(batch * tile, tile), right, preferred_element_type=F32
            )

    def weigh(wide, c_rows, result):
        def body(at, carry):
            low = pl.multiple_of(at * strip, strip)
            sums = jnp.zeros((strip, rank), F32)
            for k in range(depth):
                part = wide[pl.ds(pl.multiple_of(k * tile + low, strip), strip), :]
                sums = sums + part * c_rows[k:k + 1]
            result[pl.ds(low, strip), :] = sums
            return carry

        lax.fori_loop(0, tile // strip, body, 0)

    def along_c(s, slot):
        wide = deep_all.at[slot]
        acc_b[slot] = tile_b(s, slot).astype(F32)

        def body(at, carry):
            low = pl.multiple_of(at * strip, strip)
            rows = acc_b[slot, pl.ds(low, strip), :]
            return tuple(
                carry[k] + wide[pl.ds(pl.multiple_of(k * tile + low, strip), strip), :] * rows
                for k in range(depth)
            )

        empty = tuple(jnp.zeros((strip, rank), F32) for _ in range(depth))
        found = lax.fori_loop(0, tile // strip, body, empty)
        cc[s, r, core, slot * depth:(slot + 1) * depth, :] = jnp.concatenate(
            [jnp.sum(one, axis=0, keepdims=True) for one in found], axis=0
        )

    def wide_stage(s):
        for slot in range(slots):
            fill(spread, lambda k: bricks[slot, k:k + batch], tile_b(s, slot))
            weigh(spread, rows_c(s, slot), acc_a.at[slot])
        copies = {}
        for g in range(nc):
            at, off = g // qa, (g % qa) * ra
            da[s, g % 2, g // 2] = sum(
                w_i[slot][at] * acc_a[slot, off:off + ra, :] for slot in range(slots)
            )
        for step in list(range(1, nz)) + [0]:
            to = z_peer(step)[0]
            copies[step] = to_core(da.at[s, other, to], da1.at[s, to])
        return copies

    def deep_stage(s):
        for slot in range(slots):
            fill(deep_all.at[slot], lambda k: flip[slot, k:k + batch], tile_a(s, slot))
            along_c(s, slot)
        return spread_chips(cc.at[s, r, core])

    def drive_b_stage(s):
        for slot in range(slots):
            weigh(deep_all.at[slot], rows_c(s, slot), acc_b.at[slot])
        for g in range(nr):
            at, off = g // qb, (g % qb) * rb
            db[s, g] = sum(
                w_j[slot][at] * acc_b[slot, off:off + rb, :] for slot in range(slots)
            )
        db2[s, r] = db[s, r]
        return [
            push(db.at[s, row_peer(step)[0]], db2.at[s, r], row_peer(step)[0], c)
            for step in range(1, nr)
        ]

    def drive_a_stage(s, arriving):
        copies = []
        for step in list(range(1, nz)) + [0]:
            to = z_peer(step)[0]
            arriving[step].wait_recv()
            if step == 0:
                da2[s, z] = da[s, core, z] + da1[s, z]
            else:
                da_sum[s, to] = da[s, core, to] + da1[s, to]
                copies.append(push(da_sum.at[s, to], da2.at[s, z], r, to * 2 + core))
        return copies

    def drive_c_stage(s):
        half = spots // 2
        found = []
        for one in range(half):
            want = (r * spots + core * half + one).astype(F32)
            sums = jnp.zeros((depth, rank), F32)
            for src in range(nr):
                for side in range(2):
                    for slot in range(slots):
                        term = cc[s, src, side, slot * depth:(slot + 1) * depth, :]
                        mark = tags[src, side, slot:slot + 1, :]
                        sums = sums + jnp.where(mark == want, term, 0.0)
            found.append(sums)
        csum[s] = jnp.concatenate(found, axis=0).reshape(csum.shape[1:])
        c3[s, z] = csum[s, mine]
        copies = []
        for step in range(1, nz):
            to = z_peer(step)[0]
            copies.append(
                push(csum.at[s, to if nzc > 1 else 0], c3.at[s, z], r, to * 2 + core)
            )
        return copies

    def gram_b_stage(s):
        sb_part[s] = gram(b_all[s][...].reshape(nr * rb, rank)).reshape(sb_part.shape[1:])
        return to_core(sb_part.at[s, r, other], sb1.at[s])

    def pair_b_stage(s, arriving):
        arriving.wait_recv()
        sb2[s, z] = sb_part[s, r, core] + sb1[s]
        return [
            push(sb2.at[s, z], sb2.at[s, z], r, z_peer(step)[0] * 2 + core)
            for step in range(1, nz)
        ]

    def gram_a_stage(s):
        sa_part[s] = gram(a_all[s][...].reshape(nc * ra, rank)).reshape(sa_part.shape[1:])
        sa1[s, r] = sa_part[s, core, r]
        return [
            push(sa_part.at[s, core, row_peer(step)[0]], sa1.at[s, r], row_peer(step)[0], c)
            for step in range(1, nr)
        ]

    def prepare(state, hess):
        scale = jnp.sum(jnp.abs(hess), axis=0, keepdims=True) + 1e-06
        high = hess.astype(BF16)
        low = (hess - high.astype(F32)).astype(BF16)
        top = state.astype(BF16)
        rest = (state - top.astype(F32)).astype(BF16)
        rows = state.shape[0]
        both = jnp.dot(
            jnp.concatenate([top, rest], axis=0), high, preferred_element_type=F32
        )
        moved = both[:rows] + both[rows:] + jnp.dot(top, low, preferred_element_type=F32)
        return moved, scale

    def finish(state, ready, drive, rate):
        moved, scale = ready
        return jnp.maximum(state - rate * (moved - drive) / scale, 0.0)

    stored = []

    def keep(src, dst):
        copy = pltpu.make_async_copy(src, dst, store.at[len(stored)])
        copy.start()
        stored.append(copy)

    far_b = send_b(0)
    near_a, far_a = send_a(0)
    far_tags = spread_chips(tags.at[r, core])
    loads[2].wait()
    mine = z if nzc > 1 else 0
    start_c = r * k_row + core * k_half + mine * (k_half // nzc)
    state_c = init_c[pl.ds(pl.multiple_of(start_c, 8), k_half // nzc), :]
    c_all[0][...] = init_c[...].astype(BF16).reshape(c_all[0].shape)
    gram_c = gram(c_all[0][...].reshape(nr * k_row, rank))
    loads[3].wait()
    for slot in range(slots):
        turn(slot)
    far_c = []

    for s in range(sweeps):
        last = s == sweeps - 1
        done(far_b)
        step_sb1 = gram_b_stage(s)
        if s == 0:
            step_da1 = wide_stage(s)
            step_sb2 = pair_b_stage(s, step_sb1)
            passed_a = forward_a(s, far_a)
            step_da2 = drive_a_stage(s, step_da1)
            near_a.wait_recv()
            done(passed_a)
            step_c1 = deep_stage(s)
            step_sa1 = gram_a_stage(s)
            step_db = drive_b_stage(s)
            done(step_sb2)
            sb_full[s, r, core] = total(sb2, s, nz)
            step_sb3 = spread_row(lambda at: sb_full.at[s, at, core])
            done(step_sa1)
            sa_full[s, core, r] = total(sa1, s, nr)
            step_sa2 = spread_row(lambda at: sa_full.at[s, core, at])
            done(far_tags)
            done(step_c1)
            step_c3 = drive_c_stage(s)
        else:
            passed_a = forward_a(s, far_a)
            step_sb2 = pair_b_stage(s, step_sb1)
            done(far_c)
            wait_c = spread_chips(c_all[s].at[r, core])
            near_a.wait_recv()
            done(passed_a)
            step_c1 = deep_stage(s)
            step_sa1 = gram_a_stage(s)
            done(wait_c)
            step_da1 = wide_stage(s)
            done(step_sb2)
            sb_full[s, r, core] = total(sb2, s, nz)
            step_sb3 = spread_row(lambda at: sb_full.at[s, at, core])
            done(step_sa1)
            sa_full[s, core, r] = total(sa1, s, nr)
            step_sa2 = spread_row(lambda at: sa_full.at[s, core, at])
            done(step_c1)
            step_c3 = drive_c_stage(s)
            step_da2 = drive_a_stage(s, step_da1)
            gram_c = gram(c_all[s][...].reshape(nr * k_row, rank))
            step_db = drive_b_stage(s)
        step_sb4 = forward_row(lambda at: sb_full.at[s, at, core], step_sb3)
        step_sa3 = forward_row(lambda at: sa_full.at[s, core, at], step_sa2)
        done(step_sb4)
        gram_b = sb_full[s].reshape(rank, rank)
        if not last:
            ready_a = prepare(state_a, gram_b * gram_c)
            done(step_da2)
            state_a = finish(state_a, ready_a, total(da2, s, nz), rates[s, 0])
            a_all[s + 1][c] = state_a.astype(BF16)
            near_a, far_a = send_a(s + 1)
            done(step_sa3)
            gram_a = sa_full[s].reshape(rank, rank)
            ready_b = prepare(state_b, gram_a * gram_c)
            done(step_db)
            state_b = finish(state_b, ready_b, total(db2, s, nr), rates[s, 1])
            b_all[s + 1][r] = state_b.astype(BF16)
            far_b = send_b(s + 1)
            ready_c = prepare(state_c, gram_a * gram_b)
            done(step_c3)
            state_c = finish(state_c, ready_c, total(c3, s, nz), rates[s, 2])
            c_all[s + 1][r, core, mine] = state_c.astype(BF16)
            far_c = spread_c(lambda at: c_all[s + 1].at[r, core, at])
        else:
            done(step_sa3)
            gram_a = sa_full[s].reshape(rank, rank)
            ready_c = prepare(state_c, gram_a * gram_b)
            done(step_c3)
            final_c[r, core, mine] = finish(state_c, ready_c, total(c3, s, nz), rates[s, 2])
            far_c = spread_c(lambda at: final_c.at[r, core, at])
            ready_b = prepare(state_b, gram_a * gram_c)
            ready_a = prepare(state_a, gram_b * gram_c)
            done(far_c)
            far_c = spread_row(lambda at: final_c.at[at, core])
            done(step_db)
            init_b[...] = finish(state_b, ready_b, total(db2, s, nr), rates[s, 1])
            keep(init_b, out_b)
            done(step_da2)
            init_a[...] = finish(state_a, ready_a, total(da2, s, nz), rates[s, 0])
            keep(init_a, out_a)
            passed_c = forward_row(lambda at: final_c.at[at, core], far_c)
            for step in range(nr):
                at = row_peer(step)[1]
                keep(final_c.at[at, core], out_c.at[at, core])
            for step in range(nr):
                passed_c[step].wait_recv()
                at = row_peer(step)[1]
                keep(final_c.at[at, other], out_c.at[at, other])

    for copy in stored:
        copy.wait()
    for copy in started:
        copy.wait_send()
    assert used[0] <= sems_of


def hand_out(*arrays):
    count = len(arrays)

    def copy_all(*refs):
        copies = [
            pltpu.make_async_copy(refs[at], refs[count + at], refs[-1].at[at])
            for at in range(count)
        ]
        for copy in copies:
            copy.start()
        for copy in copies:
            copy.wait()

    far = pl.BlockSpec(memory_space=pltpu.HBM)
    return pl.pallas_call(
        copy_all,
        out_shape=tuple(jax.ShapeDtypeStruct(one.shape, one.dtype) for one in arrays),
        in_specs=[far] * count,
        out_specs=(far,) * count,
        scratch_shapes=[pltpu.SemaphoreType.DMA((count,))],
        compiler_params=pltpu.CompilerParams(vmem_limit_bytes=VMEM_BYTES),
        name="hand_out",
    )(*arrays)


def shards(nr, nc, bricks, brick_coords, brick_counts, step_sizes, init_a, init_b, init_c):
    slots, depth, tile, _ = bricks.shape[2:]
    sweeps = step_sizes.shape[0]
    ra, rank = init_a.shape[1:]
    rb = init_b.shape[1]
    depth_c = init_c.shape[0]
    nz = nc // 2
    k_row = depth_c // nr
    k_half = k_row // 2
    nzc = nz if k_half % (nz * 16) == 0 else 1
    rc = k_half // nzc
    tags = -(-slots // 8) * 8
    sems = 2 * nr + sweeps * (6 * nz + 13 * nr)
    smem = pl.BlockSpec(memory_space=pltpu.SMEM)
    far = pl.BlockSpec(memory_space=pltpu.HBM)
    scratch = [
        ((slots, depth, tile, tile), BF16),
        ((ra, rank), F32),
        ((rb, rank), F32),
        ((depth_c, rank), F32),
        ((slots, depth, tile, tile), BF16),
        [((nc, ra, rank), BF16)] * sweeps,
        [((nr, rb, rank), BF16)] * sweeps,
        [((nr, 2, nzc, rc, rank), BF16)] * sweeps,
        ((slots, tile, rank), F32),
        ((slots, tile, rank), F32),
        ((depth * tile, rank), F32),
        ((slots, depth * tile, rank), F32),
        ((nr, 2, nzc, rc, rank), F32),
        ((sweeps, 2, nz, ra, rank), F32),
        ((sweeps, nz, ra, rank), F32),
        ((sweeps, nz, ra, rank), F32),
        ((sweeps, nz, ra, rank), F32),
        ((sweeps, nr, rb, rank), F32),
        ((sweeps, nr, rb, rank), F32),
        ((sweeps, nr, 2, slots * depth, rank), F32),
        ((nr, 2, tags, rank), F32),
        ((sweeps, nzc, rc, rank), F32),
        ((sweeps, nz, rc, rank), F32),
        ((sweeps, 2, nr, rank // nr // 2, rank), F32),
        ((sweeps, nr, rank // nr // 2, rank), F32),
        ((sweeps, 2, nr, rank // nr // 2, rank), F32),
        ((sweeps, nr, 2, rank // nr // 2, rank), F32),
        ((sweeps, rank // nr // 2, rank), F32),
        ((sweeps, nz, rank // nr // 2, rank), F32),
        ((sweeps, nr, 2, rank // nr // 2, rank), F32),
    ]
    new_a, new_b, new_c = pl.pallas_call(
        functools.partial(kernel, nr, nc, sems),
        out_shape=(
            jax.ShapeDtypeStruct((ra, rank), F32),
            jax.ShapeDtypeStruct((rb, rank), F32),
            jax.ShapeDtypeStruct((nr, 2, nzc, rc, rank), F32),
        ),
        in_specs=[smem, smem, smem] + [far] * 4,
        out_specs=(far, far, far),
        scratch_shapes=[
            [pltpu.VMEM(*each) for each in one] if isinstance(one, list) else pltpu.VMEM(*one)
            for one in scratch
        ]
        + [pltpu.SemaphoreType.DMA((4,)), pltpu.SemaphoreType.DMA((2 + 2 * nr,)), pltpu.SemaphoreType.DMA((sems,)), pltpu.SemaphoreType.DMA((sems,))],
        compiler_params=pltpu.CompilerParams(
            collective_id=0, has_side_effects=True, vmem_limit_bytes=VMEM_BYTES
        ),
        name="sweeps",
    )(
        jnp.swapaxes(brick_coords, 2, 3), brick_counts, step_sizes,
        bricks.reshape(slots, depth, tile, tile), init_a[0], init_b[0], init_c,
    )
    return hand_out(new_a[None], new_b[None], new_c.reshape(depth_c, rank))


def solution(mesh):
    placed = (
        P("row", "col", None, None, None, None),
        P("row", "col", None, None),
        P("row", "col"),
        P(),
        P("row", "col", None),
        P("col", "row", None),
        P(),
    )
    return jax.shard_map(
        functools.partial(shards, mesh.shape["row"], mesh.shape["col"]),
        mesh=mesh,
        in_specs=placed,
        out_specs=(P("row", "col", None), P("col", "row", None), P()),
        check_vma=False,
    )
```

```python
import functools

import jax
import jax.numpy as jnp
from jax import lax
from jax.experimental import pallas as pl
from jax.experimental.pallas import tpu as pltpu
from jax.sharding import PartitionSpec as P

MESH = pl.DeviceIdType.MESH
F32 = jnp.float32
BF16 = jnp.bfloat16
VMEM_BYTES = 64 * 1024 * 1024 - 256 * 1024


def gram(values):
    return lax.dot_general(
        values, values, (((0,), (0,)), ((), ())), preferred_element_type=F32
    )


def kernel(
    nr, nc, sems_of,
    places, counts, rates, far_bricks, far_a0, far_b0, far_c0,
    out_a, out_b, out_c,
    bricks, init_a, init_b, init_c,
    flip, a_all, b_all, c_all, acc_a, acc_b, spread, deep_all, final_c,
    da, da1, da_sum, da2, db, db2,
    cc, tags, csum, c3,
    sa_part, sa1, sa_full, sb_part, sb1, sb2, sb_full,
    load, send, recv,
):
    nz = nc // 2
    slots, depth, tile, _ = bricks.shape
    rank = init_a.shape[-1]
    ra, rb = init_a.shape[0], init_b.shape[0]
    sweeps = rates.shape[0]
    k_row = init_c.shape[0] // nr
    k_half = k_row // 2
    spots = k_row // depth
    nzc = c_all[0].shape[2]
    qa, qb = tile // ra, tile // rb
    tiles_i, tiles_j = nc // qa, nr // qb

    loads = [
        pltpu.make_async_copy(src, dst, load.at[at])
        for at, (src, dst) in enumerate(
            ((far_b0, init_b), (far_a0, init_a), (far_c0, init_c), (far_bricks, bricks))
        )
    ]
    for copy in loads:
        copy.start()

    r = lax.axis_index("row")
    c = lax.axis_index("col")
    z = lax.div(c, 2)
    core = lax.rem(c, 2)
    other = 1 - core
    used = [0]
    started = []

    def push(src, dst, row, col):
        at = used[0]
        used[0] += 1
        copy = pltpu.make_async_remote_copy(
            src_ref=src, dst_ref=dst, send_sem=send.at[at], recv_sem=recv.at[at],
            device_id=(row, col), device_id_type=MESH,
        )
        copy.start()
        started.append(copy)
        return copy

    def to_core(src, dst):
        return push(src, dst, r, z * 2 + other)

    def row_peer(step):
        return lax.rem(r + step, nr), lax.rem(r + nr - step, nr)

    def z_peer(step):
        return lax.rem(z + step, nz), lax.rem(z + nz - step, nz)

    barrier = pltpu.get_barrier_semaphore()
    pl.semaphore_signal(barrier, inc=1, device_id=(r, z * 2 + other), device_id_type=MESH)
    for step in range(1, nr):
        pl.semaphore_signal(barrier, inc=1, device_id=(row_peer(step)[0], c), device_id_type=MESH)
    for step in range(1, nz):
        pl.semaphore_signal(
            barrier, inc=1, device_id=(r, z_peer(step)[0] * 2 + core), device_id_type=MESH
        )

    live = [counts[0, 0] > slot for slot in range(slots)]
    spot_i = [jnp.clip(places[0, 0, slot, 0], 0, tiles_i - 1) for slot in range(slots)]
    spot_j = [jnp.clip(places[0, 0, slot, 1], 0, tiles_j - 1) for slot in range(slots)]

    def weights(spot, tiles):
        return [
            [
                jnp.where(jnp.logical_and(live[slot], spot[slot] == at), 1.0, 0.0).astype(F32)
                for at in range(tiles)
            ]
            for slot in range(slots)
        ]

    w_i = weights(spot_i, tiles_i)
    w_j = weights(spot_j, tiles_j)

    spot_k = [jnp.clip(places[0, 0, slot, 2], 0, nr * spots - 1) for slot in range(slots)]
    number = lax.broadcasted_iota(jnp.int32, tags.shape[2:], 0)
    tag = jnp.full(tags.shape[2:], -1.0, F32)
    for slot in range(slots):
        mark = jnp.where(live[slot], spot_k[slot], -1).astype(F32)
        tag = jnp.where(number == slot, mark, tag)
    tags[core, r] = tag

    loads[0].wait()
    state_b = init_b[...]
    b_all[0][r] = state_b.astype(BF16)
    loads[1].wait()
    state_a = init_a[...]
    a_all[0][core, z] = state_a.astype(BF16)

    pl.semaphore_wait(barrier, 1 + (nr - 1) + (nz - 1))

    def send_b(s):
        return [push(b_all[s].at[r], b_all[s].at[r], row_peer(step)[0], c) for step in range(1, nr)]

    def send_a(s):
        mine_a = a_all[s].at[core, z]
        return [push(mine_a, mine_a, r, z_peer(step)[0] * 2 + core) for step in range(1, nz)]

    def pass_on(ref, far):
        done(far)
        return to_core(ref, ref)

    def spread_row(ref_at):
        return [push(ref_at(r), ref_at(r), row_peer(step)[0], c) for step in range(1, nr)]

    def spread_c(ref_at):
        if nzc == 1:
            return []
        return [
            push(ref_at(z), ref_at(z), r, z_peer(step)[0] * 2 + core) for step in range(1, nz)
        ]

    def done(copies):
        for copy in copies:
            copy.wait_recv()

    def total(ref, s, count):
        value = ref[s, 0]
        for at in range(1, count):
            value = value + ref[s, at]
        return value

    def turn(slot):
        def one(k, carry):
            flip[slot, k] = bricks[slot, k].T
            return carry
        lax.fori_loop(0, depth, one, 0, unroll=4)

    def tile_a(s, slot):
        half = qa // 2
        sides = [a_all[s][side, pl.ds(spot_i[slot] * half, half)] for side in range(2)]
        return jnp.stack(sides, axis=1).reshape(tile, rank)

    def tile_b(s, slot):
        return b_all[s][pl.ds(spot_j[slot] * qb, qb)].reshape(tile, rank)

    def rows_c(s, slot):
        at = spot_k[slot]
        within = lax.rem(at, spots)
        low = lax.rem(within, spots // 2)
        wide_c = c_all[s][lax.div(within, spots // 2), lax.div(at, spots)]
        flat = wide_c.astype(F32).reshape(spots // 2, depth, rank)
        picked = jnp.zeros((depth, rank), F32)
        for one in range(spots // 2):
            picked = picked + flat[one] * jnp.where(low == one, 1.0, 0.0).astype(F32)
        return picked

    strip = 8
    batch = 4

    def fill(wide, value_at, right):
        for k in range(0, depth, batch):
            wide[k * tile:(k + batch) * tile, :] = jnp.dot(
                value_at(k).reshape(batch * tile, tile), right, preferred_element_type=F32
            )

    def weigh(wide, c_rows, result):
        def body(at, carry):
            low = pl.multiple_of(at * strip, strip)
            sums = jnp.zeros((strip, rank), F32)
            for k in range(depth):
                part = wide[pl.ds(pl.multiple_of(k * tile + low, strip), strip), :]
                sums = sums + part * c_rows[k:k + 1]
            result[pl.ds(low, strip), :] = sums
            return carry

        lax.fori_loop(0, tile // strip, body, 0)

    def along_c(s, slot):
        wide = deep_all.at[slot]
        acc_b[slot] = tile_b(s, slot).astype(F32)

        def body(at, carry):
            low = pl.multiple_of(at * strip, strip)
            rows = acc_b[slot, pl.ds(low, strip), :]
            return tuple(
                carry[k] + wide[pl.ds(pl.multiple_of(k * tile + low, strip), strip), :] * rows
                for k in range(depth)
            )

        empty = tuple(jnp.zeros((strip, rank), F32) for _ in range(depth))
        found = lax.fori_loop(0, tile // strip, body, empty)
        cc[s, core, r, slot * depth:(slot + 1) * depth, :] = jnp.concatenate(
            [jnp.sum(one, axis=0, keepdims=True) for one in found], axis=0
        )

    def wide_stage(s):
        for slot in range(slots):
            fill(spread, lambda k: bricks[slot, k:k + batch], tile_b(s, slot))
            weigh(spread, rows_c(s, slot), acc_a.at[slot])
        for g in range(nc):
            at, off = g // qa, (g % qa) * ra
            da[s, g % 2, g // 2] = sum(
                w_i[slot][at] * acc_a[slot, off:off + ra, :] for slot in range(slots)
            )
        return to_core(da.at[s, other], da1.at[s])

    def deep_stage(s):
        for slot in range(slots):
            fill(deep_all.at[slot], lambda k: flip[slot, k:k + batch], tile_a(s, slot))
            along_c(s, slot)
        return spread_row(lambda at: cc.at[s, core, at])

    def drive_b_stage(s):
        for slot in range(slots):
            weigh(deep_all.at[slot], rows_c(s, slot), acc_b.at[slot])
        for g in range(nr):
            at, off = g // qb, (g % qb) * rb
            db[s, g] = sum(
                w_j[slot][at] * acc_b[slot, off:off + rb, :] for slot in range(slots)
            )
        db2[s, r] = db[s, r]
        return [
            push(db.at[s, row_peer(step)[0]], db2.at[s, r], row_peer(step)[0], c)
            for step in range(1, nr)
        ]

    def drive_a_stage(s, arriving):
        copies = []
        arriving.wait_recv()
        for step in list(range(1, nz)) + [0]:
            to = z_peer(step)[0]
            if step == 0:
                da2[s, z] = da[s, core, z] + da1[s, z]
            else:
                da_sum[s, to] = da[s, core, to] + da1[s, to]
                copies.append(push(da_sum.at[s, to], da2.at[s, z], r, to * 2 + core))
        return copies

    def drive_c_stage(s):
        half = spots // 2
        found = []
        for one in range(half):
            want = (r * spots + core * half + one).astype(F32)
            sums = jnp.zeros((depth, rank), F32)
            for src in range(nr):
                for side in range(2):
                    for slot in range(slots):
                        term = cc[s, side, src, slot * depth:(slot + 1) * depth, :]
                        mark = tags[side, src, slot:slot + 1, :]
                        sums = sums + jnp.where(mark == want, term, 0.0)
            found.append(sums)
        csum[s] = jnp.concatenate(found, axis=0).reshape(csum.shape[1:])
        c3[s, z] = csum[s, mine]
        copies = []
        for step in range(1, nz):
            to = z_peer(step)[0]
            copies.append(
                push(csum.at[s, to if nzc > 1 else 0], c3.at[s, z], r, to * 2 + core)
            )
        return copies

    def gram_b_stage(s):
        sb_part[s] = gram(b_all[s][...].reshape(nr * rb, rank)).reshape(sb_part.shape[1:])
        return to_core(sb_part.at[s, r, other], sb1.at[s])

    def pair_b_stage(s, arriving):
        arriving.wait_recv()
        sb2[s, z] = sb_part[s, r, core] + sb1[s]
        return [
            push(sb2.at[s, z], sb2.at[s, z], r, z_peer(step)[0] * 2 + core)
            for step in range(1, nz)
        ]

    def gram_a_stage(s):
        sa_part[s] = gram(a_all[s][...].reshape(nc * ra, rank)).reshape(sa_part.shape[1:])
        sa1[s, r] = sa_part[s, core, r]
        return [
            push(sa_part.at[s, core, row_peer(step)[0]], sa1.at[s, r], row_peer(step)[0], c)
            for step in range(1, nr)
        ]

    def prepare(state, hess):
        scale = jnp.sum(jnp.abs(hess), axis=0, keepdims=True) + 1e-06
        high = hess.astype(BF16)
        low = (hess - high.astype(F32)).astype(BF16)
        top = state.astype(BF16)
        rest = (state - top.astype(F32)).astype(BF16)
        rows = state.shape[0]
        both = jnp.dot(
            jnp.concatenate([top, rest], axis=0), high, preferred_element_type=F32
        )
        moved = both[:rows] + both[rows:] + jnp.dot(top, low, preferred_element_type=F32)
        return moved, scale

    def finish(state, ready, drive, rate):
        moved, scale = ready
        return state - rate * (moved - drive) / scale

    far_b = send_b(0)
    far_a = send_a(0)
    far_tags = spread_row(lambda at: tags.at[core, at])
    loads[2].wait()
    mine = z if nzc > 1 else 0
    start_c = r * k_row + core * k_half + mine * (k_half // nzc)
    state_c = init_c[pl.ds(pl.multiple_of(start_c, 8), k_half // nzc), :]
    for at in range(nr):
        for side in range(2):
            low = at * k_row + side * k_half
            c_all[0][side, at] = init_c[low:low + k_half, :].astype(BF16).reshape(
                c_all[0].shape[2:]
            )
    gram_c = gram(c_all[0][...].reshape(nr * k_row, rank))
    loads[3].wait()
    for slot in range(slots):
        turn(slot)
    far_c = []

    for s in range(sweeps):
        last = s == sweeps - 1
        first = s == 0
        done(far_b)
        step_sb1 = gram_b_stage(s)
        if first:
            step_da1 = wide_stage(s)
        near_a = pass_on(a_all[s].at[core], far_a)
        step_sb2 = pair_b_stage(s, step_sb1)
        if first:
            step_da2 = drive_a_stage(s, step_da1)
        else:
            done(far_c)
            far_c = spread_row(lambda at: c_all[s].at[core, at])
        near_a.wait_recv()
        step_c1 = deep_stage(s)
        step_sa1 = gram_a_stage(s)
        if first:
            near_tags = pass_on(tags.at[core], far_tags)
        else:
            near_c = pass_on(c_all[s].at[core], far_c)
        near_cc = pass_on(cc.at[s, core], step_c1)
        if not first:
            near_c.wait_recv()
            step_da1 = wide_stage(s)
        done(step_sa1)
        sa_full[s, core, r] = total(sa1, s, nr)
        step_sa2 = spread_row(lambda at: sa_full.at[s, core, at])
        done(step_sb2)
        sb_full[s, core, r] = total(sb2, s, nz)
        step_sb3 = spread_row(lambda at: sb_full.at[s, core, at])
        if first:
            near_tags.wait_recv()
        near_cc.wait_recv()
        step_c3 = drive_c_stage(s)
        if not first:
            step_da2 = drive_a_stage(s, step_da1)
            gram_c = gram(c_all[s][...].reshape(nr * k_row, rank))
        step_db = drive_b_stage(s)
        near_sa = pass_on(sa_full.at[s, core], step_sa2)
        near_sb = pass_on(sb_full.at[s, core], step_sb3)
        near_sb.wait_recv()
        gram_b = jnp.stack([sb_full[s, side] for side in range(2)], axis=1).reshape(rank, rank)
        if not last:
            ready_a = prepare(state_a, gram_b * gram_c)
            done(step_da2)
            state_a = jnp.maximum(finish(state_a, ready_a, total(da2, s, nz), rates[s, 0]), 0.0)
            a_all[s + 1][core, z] = state_a.astype(BF16)
            far_a = send_a(s + 1)
            near_sa.wait_recv()
            gram_a = sa_full[s].reshape(rank, rank)
            ready_b = prepare(state_b, gram_a * gram_c)
            done(step_db)
            state_b = jnp.maximum(finish(state_b, ready_b, total(db2, s, nr), rates[s, 1]), 0.0)
            b_all[s + 1][r] = state_b.astype(BF16)
            far_b = send_b(s + 1)
            ready_c = prepare(state_c, gram_a * gram_b)
            done(step_c3)
            state_c = jnp.maximum(finish(state_c, ready_c, total(c3, s, nz), rates[s, 2]), 0.0)
            c_all[s + 1][core, r, mine] = state_c.astype(BF16)
            far_c = spread_c(lambda at: c_all[s + 1].at[core, r, at])
        else:
            near_sa.wait_recv()
            gram_a = sa_full[s].reshape(rank, rank)
            ready_c = prepare(state_c, gram_a * gram_b)
            done(step_c3)
            final_c[core, r, mine] = finish(state_c, ready_c, total(c3, s, nz), rates[s, 2])
            far_c = spread_c(lambda at: final_c.at[core, r, at])
            ready_b = prepare(state_b, gram_a * gram_c)
            ready_a = prepare(state_a, gram_b * gram_c)
            done(far_c)
            far_c = spread_row(lambda at: final_c.at[core, at])
            done(step_db)
            out_b[...] = finish(state_b, ready_b, total(db2, s, nr), rates[s, 1])
            done(step_da2)
            out_a[...] = finish(state_a, ready_a, total(da2, s, nz), rates[s, 0])
            near_c = pass_on(final_c.at[core], far_c)
            for at in range(nr):
                out_c[at, core] = final_c[core, at]
            near_c.wait_recv()
            for at in range(nr):
                out_c[at, other] = final_c[other, at]

    for copy in started:
        copy.wait_send()
    assert used[0] <= sems_of


def clamp(values):
    return jnp.maximum(values, 0.0)


def shards(nr, nc, bricks, brick_coords, brick_counts, step_sizes, init_a, init_b, init_c):
    slots, depth, tile, _ = bricks.shape[2:]
    sweeps = step_sizes.shape[0]
    ra, rank = init_a.shape[1:]
    rb = init_b.shape[1]
    depth_c = init_c.shape[0]
    nz = nc // 2
    k_row = depth_c // nr
    k_half = k_row // 2
    nzc = nz if k_half % (nz * 16) == 0 else 1
    rc = k_half // nzc
    tags = -(-slots // 8) * 8
    sems = 2 * nr + sweeps * (6 * nz + 13 * nr)
    smem = pl.BlockSpec(memory_space=pltpu.SMEM)
    far = pl.BlockSpec(memory_space=pltpu.HBM)
    vmem = pl.BlockSpec(memory_space=pltpu.VMEM)
    scratch = [
        ((slots, depth, tile, tile), BF16),
        ((ra, rank), F32),
        ((rb, rank), F32),
        ((depth_c, rank), F32),
        ((slots, depth, tile, tile), BF16),
        [((2, nz, ra, rank), BF16)] * sweeps,
        [((nr, rb, rank), BF16)] * sweeps,
        [((2, nr, nzc, rc, rank), BF16)] * sweeps,
        ((slots, tile, rank), F32),
        ((slots, tile, rank), F32),
        ((depth * tile, rank), F32),
        ((slots, depth * tile, rank), F32),
        ((2, nr, nzc, rc, rank), F32),
        ((sweeps, 2, nz, ra, rank), F32),
        ((sweeps, nz, ra, rank), F32),
        ((sweeps, nz, ra, rank), F32),
        ((sweeps, nz, ra, rank), F32),
        ((sweeps, nr, rb, rank), F32),
        ((sweeps, nr, rb, rank), F32),
        ((sweeps, 2, nr, slots * depth, rank), F32),
        ((2, nr, tags, rank), F32),
        ((sweeps, nzc, rc, rank), F32),
        ((sweeps, nz, rc, rank), F32),
        ((sweeps, 2, nr, rank // nr // 2, rank), F32),
        ((sweeps, nr, rank // nr // 2, rank), F32),
        ((sweeps, 2, nr, rank // nr // 2, rank), F32),
        ((sweeps, nr, 2, rank // nr // 2, rank), F32),
        ((sweeps, rank // nr // 2, rank), F32),
        ((sweeps, nz, rank // nr // 2, rank), F32),
        ((sweeps, 2, nr, rank // nr // 2, rank), F32),
    ]
    new_a, new_b, new_c = pl.pallas_call(
        functools.partial(kernel, nr, nc, sems),
        out_shape=(
            jax.ShapeDtypeStruct((ra, rank), F32),
            jax.ShapeDtypeStruct((rb, rank), F32),
            jax.ShapeDtypeStruct((nr, 2, nzc, rc, rank), F32),
        ),
        in_specs=[smem, smem, smem] + [far] * 4,
        out_specs=(vmem, vmem, vmem),
        scratch_shapes=[
            [pltpu.VMEM(*each) for each in one] if isinstance(one, list) else pltpu.VMEM(*one)
            for one in scratch
        ]
        + [pltpu.SemaphoreType.DMA((4,)), pltpu.SemaphoreType.DMA((sems,)), pltpu.SemaphoreType.DMA((sems,))],
        compiler_params=pltpu.CompilerParams(
            collective_id=0, has_side_effects=True, vmem_limit_bytes=VMEM_BYTES
        ),
        name="sweeps",
    )(
        jnp.swapaxes(brick_coords, 2, 3), brick_counts, step_sizes,
        bricks.reshape(slots, depth, tile, tile), init_a[0], init_b[0], init_c,
    )
    return clamp(new_a)[None], clamp(new_b)[None], clamp(new_c.reshape(depth_c, rank))


def solution(mesh):
    placed = (
        P("row", "col", None, None, None, None),
        P("row", "col", None, None),
        P("row", "col"),
        P(),
        P("row", "col", None),
        P("col", "row", None),
        P(),
    )
    return jax.shard_map(
        functools.partial(shards, mesh.shape["row"], mesh.shape["col"]),
        mesh=mesh,
        in_specs=placed,
        out_specs=(P("row", "col", None), P("col", "row", None), P()),
        check_vma=False,
    )
```

```python
import functools

import jax
import jax.numpy as jnp
from jax import lax
from jax.experimental import pallas as pl
from jax.experimental.pallas import tpu as pltpu
from jax.sharding import PartitionSpec as P

MESH = pl.DeviceIdType.MESH
F32 = jnp.float32
BF16 = jnp.bfloat16
VMEM_BYTES = 64 * 1024 * 1024 - 256 * 1024


def gram(values):
    return lax.dot_general(
        values, values, (((0,), (0,)), ((), ())), preferred_element_type=F32
    )


def kernel(
    nr, nc, sems_of,
    places, counts, rates, far_bricks, far_a0, far_b0, far_c0,
    out_a, out_b, out_c,
    bricks, init_a, init_b, init_c,
    flip, a_all, b_all, c_all, acc_a, acc_b, spread, deep_all, final_c,
    da, da1, da_sum, da2, db, db2,
    cc, tags, csum, c3,
    sa_part, sa1, sa_full, sb_part, sb1, sb2, sb_full,
    load, send, recv,
):
    nz = nc // 2
    slots, depth, tile, _ = bricks.shape
    rank = init_a.shape[-1]
    ra, rb = init_a.shape[0], init_b.shape[0]
    sweeps = rates.shape[0]
    k_row = init_c.shape[0] // nr
    k_half = k_row // 2
    spots = k_row // depth
    nzc = c_all[0].shape[2]
    qa, qb = tile // ra, tile // rb
    tiles_i, tiles_j = nc // qa, nr // qb

    loads = [
        pltpu.make_async_copy(src, dst, load.at[at])
        for at, (src, dst) in enumerate(
            ((far_b0, init_b), (far_a0, init_a), (far_c0, init_c), (far_bricks, bricks))
        )
    ]
    for copy in loads:
        copy.start()

    r = lax.axis_index("row")
    c = lax.axis_index("col")
    z = lax.div(c, 2)
    core = lax.rem(c, 2)
    other = 1 - core
    used = [0]
    started = []

    def push(src, dst, row, col):
        at = used[0]
        used[0] += 1
        copy = pltpu.make_async_remote_copy(
            src_ref=src, dst_ref=dst, send_sem=send.at[at], recv_sem=recv.at[at],
            device_id=(row, col), device_id_type=MESH,
        )
        copy.start()
        started.append(copy)
        return copy

    def to_core(src, dst):
        return push(src, dst, r, z * 2 + other)

    def row_peer(step):
        return lax.rem(r + step, nr), lax.rem(r + nr - step, nr)

    def z_peer(step):
        return lax.rem(z + step, nz), lax.rem(z + nz - step, nz)

    barrier = pltpu.get_barrier_semaphore()
    pl.semaphore_signal(barrier, inc=1, device_id=(r, z * 2 + other), device_id_type=MESH)
    for step in range(1, nr):
        pl.semaphore_signal(barrier, inc=1, device_id=(row_peer(step)[0], c), device_id_type=MESH)
    for step in range(1, nz):
        pl.semaphore_signal(
            barrier, inc=1, device_id=(r, z_peer(step)[0] * 2 + core), device_id_type=MESH
        )

    live = [counts[0, 0] > slot for slot in range(slots)]
    spot_i = [jnp.clip(places[0, 0, slot, 0], 0, tiles_i - 1) for slot in range(slots)]
    spot_j = [jnp.clip(places[0, 0, slot, 1], 0, tiles_j - 1) for slot in range(slots)]

    def weights(spot, tiles):
        return [
            [
                jnp.where(jnp.logical_and(live[slot], spot[slot] == at), 1.0, 0.0).astype(F32)
                for at in range(tiles)
            ]
            for slot in range(slots)
        ]

    w_i = weights(spot_i, tiles_i)
    w_j = weights(spot_j, tiles_j)

    spot_k = [jnp.clip(places[0, 0, slot, 2], 0, nr * spots - 1) for slot in range(slots)]
    number = lax.broadcasted_iota(jnp.int32, tags.shape[2:], 0)
    tag = jnp.full(tags.shape[2:], -1.0, F32)
    for slot in range(slots):
        mark = jnp.where(live[slot], spot_k[slot], -1).astype(F32)
        tag = jnp.where(number == slot, mark, tag)
    tags[core, r] = tag

    loads[0].wait()
    state_b = init_b[...]
    b_all[0][r] = state_b.astype(BF16)
    loads[1].wait()
    state_a = init_a[...]
    a_all[0][core, z] = state_a.astype(BF16)

    pl.semaphore_wait(barrier, 1 + (nr - 1) + (nz - 1))

    def send_b(s):
        return [push(b_all[s].at[r], b_all[s].at[r], row_peer(step)[0], c) for step in range(1, nr)]

    def send_a(s):
        mine_a = a_all[s].at[core, z]
        return [push(mine_a, mine_a, r, z_peer(step)[0] * 2 + core) for step in range(1, nz)]

    def pass_on(ref, far):
        done(far)
        return to_core(ref, ref)

    def spread_row(ref_at):
        return [push(ref_at(r), ref_at(r), row_peer(step)[0], c) for step in range(1, nr)]

    def spread_c(ref_at):
        if nzc == 1:
            return []
        return [
            push(ref_at(z), ref_at(z), r, z_peer(step)[0] * 2 + core) for step in range(1, nz)
        ]

    def done(copies):
        for copy in copies:
            copy.wait_recv()

    def total(ref, s, count):
        value = ref[s, 0]
        for at in range(1, count):
            value = value + ref[s, at]
        return value

    def turn(slot):
        def one(k, carry):
            flip[slot, k] = bricks[slot, k].T
            return carry
        lax.fori_loop(0, depth, one, 0, unroll=4)

    def tile_a(s, slot):
        half = qa // 2
        sides = [a_all[s][side, pl.ds(spot_i[slot] * half, half)] for side in range(2)]
        return jnp.stack(sides, axis=1).reshape(tile, rank)

    def tile_b(s, slot):
        return b_all[s][pl.ds(spot_j[slot] * qb, qb)].reshape(tile, rank)

    def rows_c(s, slot):
        at = spot_k[slot]
        within = lax.rem(at, spots)
        low = lax.rem(within, spots // 2)
        wide_c = c_all[s][lax.div(within, spots // 2), lax.div(at, spots)]
        flat = wide_c.astype(F32).reshape(spots // 2, depth, rank)
        picked = jnp.zeros((depth, rank), F32)
        for one in range(spots // 2):
            picked = picked + flat[one] * jnp.where(low == one, 1.0, 0.0).astype(F32)
        return picked

    strip = 8
    batch = 4

    def fill(wide, value_at, right):
        for k in range(0, depth, batch):
            wide[k * tile:(k + batch) * tile, :] = jnp.dot(
                value_at(k).reshape(batch * tile, tile), right, preferred_element_type=F32
            )

    def weigh(wide, c_rows, result):
        def body(at, carry):
            low = pl.multiple_of(at * strip, strip)
            sums = jnp.zeros((strip, rank), F32)
            for k in range(depth):
                part = wide[pl.ds(pl.multiple_of(k * tile + low, strip), strip), :]
                sums = sums + part * c_rows[k:k + 1]
            result[pl.ds(low, strip), :] = sums
            return carry

        lax.fori_loop(0, tile // strip, body, 0)

    def along_c(s, slot):
        wide = deep_all.at[slot]
        acc_b[slot] = tile_b(s, slot).astype(F32)

        def body(at, carry):
            low = pl.multiple_of(at * strip, strip)
            rows = acc_b[slot, pl.ds(low, strip), :]
            return tuple(
                carry[k] + wide[pl.ds(pl.multiple_of(k * tile + low, strip), strip), :] * rows
                for k in range(depth)
            )

        empty = tuple(jnp.zeros((strip, rank), F32) for _ in range(depth))
        found = lax.fori_loop(0, tile // strip, body, empty)
        cc[s, core, r, slot * depth:(slot + 1) * depth, :] = jnp.concatenate(
            [jnp.sum(one, axis=0, keepdims=True) for one in found], axis=0
        )

    def wide_stage(s):
        for slot in range(slots):
            fill(spread, lambda k: bricks[slot, k:k + batch], tile_b(s, slot))
            weigh(spread, rows_c(s, slot), acc_a.at[slot])
        for g in range(nc):
            at, off = g // qa, (g % qa) * ra
            da[s, g % 2, g // 2] = sum(
                w_i[slot][at] * acc_a[slot, off:off + ra, :] for slot in range(slots)
            )
        return to_core(da.at[s, other], da1.at[s])

    def deep_stage(s, between):
        for slot in range(slots):
            fill(deep_all.at[slot], lambda k: flip[slot, k:k + batch], tile_a(s, slot))
            along_c(s, slot)
            if slot == 0:
                between()
        return spread_row(lambda at: cc.at[s, core, at])

    def drive_b_stage(s):
        for slot in range(slots):
            weigh(deep_all.at[slot], rows_c(s, slot), acc_b.at[slot])
        for g in range(nr):
            at, off = g // qb, (g % qb) * rb
            db[s, g] = sum(
                w_j[slot][at] * acc_b[slot, off:off + rb, :] for slot in range(slots)
            )
        db2[s, r] = db[s, r]
        return [
            push(db.at[s, row_peer(step)[0]], db2.at[s, r], row_peer(step)[0], c)
            for step in range(1, nr)
        ]

    def drive_a_stage(s, arriving):
        copies = []
        arriving.wait_recv()
        for step in list(range(1, nz)) + [0]:
            to = z_peer(step)[0]
            if step == 0:
                da2[s, z] = da[s, core, z] + da1[s, z]
            else:
                da_sum[s, to] = da[s, core, to] + da1[s, to]
                copies.append(push(da_sum.at[s, to], da2.at[s, z], r, to * 2 + core))
        return copies

    def drive_c_stage(s):
        half = spots // 2
        found = []
        for one in range(half):
            want = (r * spots + core * half + one).astype(F32)
            sums = jnp.zeros((depth, rank), F32)
            for src in range(nr):
                for side in range(2):
                    for slot in range(slots):
                        term = cc[s, side, src, slot * depth:(slot + 1) * depth, :]
                        mark = tags[side, src, slot:slot + 1, :]
                        sums = sums + jnp.where(mark == want, term, 0.0)
            found.append(sums)
        csum[s] = jnp.concatenate(found, axis=0).reshape(csum.shape[1:])
        c3[s, z] = csum[s, mine]
        copies = []
        for step in range(1, nz):
            to = z_peer(step)[0]
            copies.append(
                push(csum.at[s, to if nzc > 1 else 0], c3.at[s, z], r, to * 2 + core)
            )
        return copies

    def gram_b_stage(s):
        sb_part[s] = gram(b_all[s][...].reshape(nr * rb, rank)).reshape(sb_part.shape[1:])
        return to_core(sb_part.at[s, r, other], sb1.at[s])

    def pair_b_stage(s, arriving):
        arriving.wait_recv()
        sb2[s, z] = sb_part[s, r, core] + sb1[s]
        return [
            push(sb2.at[s, z], sb2.at[s, z], r, z_peer(step)[0] * 2 + core)
            for step in range(1, nz)
        ]

    def gram_a_stage(s):
        sa_part[s] = gram(a_all[s][...].reshape(nc * ra, rank)).reshape(sa_part.shape[1:])
        sa1[s, r] = sa_part[s, core, r]
        return [
            push(sa_part.at[s, core, row_peer(step)[0]], sa1.at[s, r], row_peer(step)[0], c)
            for step in range(1, nr)
        ]

    def prepare(state, hess):
        scale = jnp.sum(jnp.abs(hess), axis=0, keepdims=True) + 1e-06
        high = hess.astype(BF16)
        low = (hess - high.astype(F32)).astype(BF16)
        top = state.astype(BF16)
        rest = (state - top.astype(F32)).astype(BF16)
        rows = state.shape[0]
        both = jnp.dot(
            jnp.concatenate([top, rest], axis=0), high, preferred_element_type=F32
        )
        moved = both[:rows] + both[rows:] + jnp.dot(top, low, preferred_element_type=F32)
        return moved, scale

    def finish(state, ready, drive, rate):
        moved, scale = ready
        return state - rate * (moved - drive) / scale

    far_b = send_b(0)
    far_a = send_a(0)
    far_tags = spread_row(lambda at: tags.at[core, at])
    loads[2].wait()
    mine = z if nzc > 1 else 0
    start_c = r * k_row + core * k_half + mine * (k_half // nzc)
    state_c = init_c[pl.ds(pl.multiple_of(start_c, 8), k_half // nzc), :]
    for at in range(nr):
        for side in range(2):
            low = at * k_row + side * k_half
            c_all[0][side, at] = init_c[low:low + k_half, :].astype(BF16).reshape(
                c_all[0].shape[2:]
            )
    gram_c = gram(c_all[0][...].reshape(nr * k_row, rank))
    loads[3].wait()
    for slot in range(slots):
        turn(slot)
    far_c = []

    for s in range(sweeps):
        last = s == sweeps - 1
        first = s == 0
        late = {}

        def sum_b():
            done(step_sb2)
            sb_full[s, core, r] = total(sb2, s, nz)
            late["sb3"] = spread_row(lambda at: sb_full.at[s, core, at])

        def move_c():
            done(far_c)
            late["c"] = spread_row(lambda at: c_all[s].at[core, at])

        if first:
            done(far_b)
            step_sb1 = gram_b_stage(s)
            step_da1 = wide_stage(s)
            near_a = pass_on(a_all[s].at[core], far_a)
            step_sb2 = pair_b_stage(s, step_sb1)
            step_da2 = drive_a_stage(s, step_da1)
            near_a.wait_recv()
            step_sa1 = gram_a_stage(s)
            step_c1 = deep_stage(s, sum_b)
            step_db = drive_b_stage(s)
            done(step_sa1)
            sa_full[s, core, r] = total(sa1, s, nr)
            step_sa2 = spread_row(lambda at: sa_full.at[s, core, at])
            near_sb = pass_on(sb_full.at[s, core], late["sb3"])
            near_tags = pass_on(tags.at[core], far_tags)
            near_cc = pass_on(cc.at[s, core], step_c1)
        else:
            near_a = pass_on(a_all[s].at[core], far_a)
            done(far_b)
            step_sb1 = gram_b_stage(s)
            near_a.wait_recv()
            step_c1 = deep_stage(s, move_c)
            step_sb2 = pair_b_stage(s, step_sb1)
            step_sa1 = gram_a_stage(s)
            near_c = pass_on(c_all[s].at[core], late["c"])
            near_cc = pass_on(cc.at[s, core], step_c1)
            done(step_sa1)
            sa_full[s, core, r] = total(sa1, s, nr)
            step_sa2 = spread_row(lambda at: sa_full.at[s, core, at])
            near_c.wait_recv()
            step_da1 = wide_stage(s)
            near_cc.wait_recv()
            step_c3 = drive_c_stage(s)
            sum_b()
            step_da2 = drive_a_stage(s, step_da1)
            gram_c = gram(c_all[s][...].reshape(nr * k_row, rank))
            near_sa = pass_on(sa_full.at[s, core], step_sa2)
            step_db = drive_b_stage(s)
            near_sb = pass_on(sb_full.at[s, core], late["sb3"])
        near_sb.wait_recv()
        gram_b = jnp.stack([sb_full[s, side] for side in range(2)], axis=1).reshape(rank, rank)
        if not last:
            ready_a = prepare(state_a, gram_b * gram_c)
            done(step_da2)
            state_a = jnp.maximum(finish(state_a, ready_a, total(da2, s, nz), rates[s, 0]), 0.0)
            a_all[s + 1][core, z] = state_a.astype(BF16)
            far_a = send_a(s + 1)
            near_sa = pass_on(sa_full.at[s, core], step_sa2)
            near_tags.wait_recv()
            near_cc.wait_recv()
            step_c3 = drive_c_stage(s)
            near_sa.wait_recv()
            gram_a = sa_full[s].reshape(rank, rank)
            ready_b = prepare(state_b, gram_a * gram_c)
            done(step_db)
            state_b = jnp.maximum(finish(state_b, ready_b, total(db2, s, nr), rates[s, 1]), 0.0)
            b_all[s + 1][r] = state_b.astype(BF16)
            far_b = send_b(s + 1)
            ready_c = prepare(state_c, gram_a * gram_b)
            done(step_c3)
            state_c = jnp.maximum(finish(state_c, ready_c, total(c3, s, nz), rates[s, 2]), 0.0)
            c_all[s + 1][core, r, mine] = state_c.astype(BF16)
            far_c = spread_c(lambda at: c_all[s + 1].at[core, r, at])
        else:
            near_sa.wait_recv()
            gram_a = sa_full[s].reshape(rank, rank)
            ready_c = prepare(state_c, gram_a * gram_b)
            done(step_c3)
            final_c[core, r, mine] = finish(state_c, ready_c, total(c3, s, nz), rates[s, 2])
            far_c = spread_c(lambda at: final_c.at[core, r, at])
            ready_b = prepare(state_b, gram_a * gram_c)
            ready_a = prepare(state_a, gram_b * gram_c)
            done(far_c)
            far_c = spread_row(lambda at: final_c.at[core, at])
            done(step_db)
            out_b[...] = finish(state_b, ready_b, total(db2, s, nr), rates[s, 1])
            done(step_da2)
            out_a[...] = finish(state_a, ready_a, total(da2, s, nz), rates[s, 0])
            near_c = pass_on(final_c.at[core], far_c)
            for at in range(nr):
                out_c[at, core] = final_c[core, at]
            near_c.wait_recv()
            for at in range(nr):
                out_c[at, other] = final_c[other, at]

    for copy in started:
        copy.wait_send()
    assert used[0] <= sems_of


def clamp(values):
    return jnp.maximum(values, 0.0)


def shards(nr, nc, bricks, brick_coords, brick_counts, step_sizes, init_a, init_b, init_c):
    slots, depth, tile, _ = bricks.shape[2:]
    sweeps = step_sizes.shape[0]
    ra, rank = init_a.shape[1:]
    rb = init_b.shape[1]
    depth_c = init_c.shape[0]
    nz = nc // 2
    k_row = depth_c // nr
    k_half = k_row // 2
    nzc = nz if k_half % (nz * 16) == 0 else 1
    rc = k_half // nzc
    tags = -(-slots // 8) * 8
    sems = 2 * nr + sweeps * (6 * nz + 13 * nr)
    smem = pl.BlockSpec(memory_space=pltpu.SMEM)
    far = pl.BlockSpec(memory_space=pltpu.HBM)
    vmem = pl.BlockSpec(memory_space=pltpu.VMEM)
    scratch = [
        ((slots, depth, tile, tile), BF16),
        ((ra, rank), F32),
        ((rb, rank), F32),
        ((depth_c, rank), F32),
        ((slots, depth, tile, tile), BF16),
        [((2, nz, ra, rank), BF16)] * sweeps,
        [((nr, rb, rank), BF16)] * sweeps,
        [((2, nr, nzc, rc, rank), BF16)] * sweeps,
        ((slots, tile, rank), F32),
        ((slots, tile, rank), F32),
        ((depth * tile, rank), F32),
        ((slots, depth * tile, rank), F32),
        ((2, nr, nzc, rc, rank), F32),
        ((sweeps, 2, nz, ra, rank), F32),
        ((sweeps, nz, ra, rank), F32),
        ((sweeps, nz, ra, rank), F32),
        ((sweeps, nz, ra, rank), F32),
        ((sweeps, nr, rb, rank), F32),
        ((sweeps, nr, rb, rank), F32),
        ((sweeps, 2, nr, slots * depth, rank), F32),
        ((2, nr, tags, rank), F32),
        ((sweeps, nzc, rc, rank), F32),
        ((sweeps, nz, rc, rank), F32),
        ((sweeps, 2, nr, rank // nr // 2, rank), F32),
        ((sweeps, nr, rank // nr // 2, rank), F32),
        ((sweeps, 2, nr, rank // nr // 2, rank), F32),
        ((sweeps, nr, 2, rank // nr // 2, rank), F32),
        ((sweeps, rank // nr // 2, rank), F32),
        ((sweeps, nz, rank // nr // 2, rank), F32),
        ((sweeps, 2, nr, rank // nr // 2, rank), F32),
    ]
    new_a, new_b, new_c = pl.pallas_call(
        functools.partial(kernel, nr, nc, sems),
        out_shape=(
            jax.ShapeDtypeStruct((ra, rank), F32),
            jax.ShapeDtypeStruct((rb, rank), F32),
            jax.ShapeDtypeStruct((nr, 2, nzc, rc, rank), F32),
        ),
        in_specs=[smem, smem, smem] + [far] * 4,
        out_specs=(vmem, vmem, vmem),
        scratch_shapes=[
            [pltpu.VMEM(*each) for each in one] if isinstance(one, list) else pltpu.VMEM(*one)
            for one in scratch
        ]
        + [pltpu.SemaphoreType.DMA((4,)), pltpu.SemaphoreType.DMA((sems,)), pltpu.SemaphoreType.DMA((sems,))],
        compiler_params=pltpu.CompilerParams(
            collective_id=0, has_side_effects=True, vmem_limit_bytes=VMEM_BYTES
        ),
        name="sweeps",
    )(
        jnp.swapaxes(brick_coords, 2, 3), brick_counts, step_sizes,
        bricks.reshape(slots, depth, tile, tile), init_a[0], init_b[0], init_c,
    )
    return clamp(new_a)[None], clamp(new_b)[None], clamp(new_c.reshape(depth_c, rank))


def solution(mesh):
    placed = (
        P("row", "col", None, None, None, None),
        P("row", "col", None, None),
        P("row", "col"),
        P(),
        P("row", "col", None),
        P("col", "row", None),
        P(),
    )
    return jax.shard_map(
        functools.partial(shards, mesh.shape["row"], mesh.shape["col"]),
        mesh=mesh,
        in_specs=placed,
        out_specs=(P("row", "col", None), P("col", "row", None), P()),
        check_vma=False,
    )
```

```python
import functools

import jax
import jax.numpy as jnp
from jax import lax
from jax.experimental import pallas as pl
from jax.experimental.pallas import tpu as pltpu
from jax.sharding import PartitionSpec as P

MESH = pl.DeviceIdType.MESH
F32 = jnp.float32
BF16 = jnp.bfloat16
VMEM_BYTES = 64 * 1024 * 1024 - 256 * 1024


def gram(values):
    return lax.dot_general(
        values, values, (((0,), (0,)), ((), ())), preferred_element_type=F32
    )


def kernel(
    nr, nc, sems_of,
    places, counts, rates, far_bricks, far_a0, far_b0, far_c0,
    out_a, out_b, out_c,
    bricks, init_a, init_b, init_c,
    flip, a_all, b_all, c_all, acc_a, acc_b, spread, deep_all, final_c,
    da, da1, da_sum, da2, db, db2,
    cc, tags, csum, c3,
    sa_part, sa1, sa_full, sb_part, sb1, sb2, sb_full,
    load, send, recv,
):
    nz = nc // 2
    slots, depth, tile, _ = bricks.shape
    rank = init_a.shape[-1]
    ra, rb = init_a.shape[0], init_b.shape[0]
    sweeps = rates.shape[0]
    k_row = init_c.shape[0] // nr
    k_half = k_row // 2
    spots = k_row // depth
    nzc = c_all[0].shape[2]
    qa, qb = tile // ra, tile // rb
    tiles_i, tiles_j = nc // qa, nr // qb

    loads = [
        pltpu.make_async_copy(src, dst, load.at[at])
        for at, (src, dst) in enumerate(
            ((far_b0, init_b), (far_a0, init_a), (far_c0, init_c), (far_bricks, bricks))
        )
    ]
    for copy in loads:
        copy.start()

    r = lax.axis_index("row")
    c = lax.axis_index("col")
    z = lax.div(c, 2)
    core = lax.rem(c, 2)
    other = 1 - core
    used = [0]
    started = []

    def push(src, dst, row, col):
        at = used[0]
        used[0] += 1
        copy = pltpu.make_async_remote_copy(
            src_ref=src, dst_ref=dst, send_sem=send.at[at], recv_sem=recv.at[at],
            device_id=(row, col), device_id_type=MESH,
        )
        copy.start()
        started.append(copy)
        return copy

    def to_core(src, dst):
        return push(src, dst, r, z * 2 + other)

    def row_peer(step):
        return lax.rem(r + step, nr), lax.rem(r + nr - step, nr)

    def z_peer(step):
        return lax.rem(z + step, nz), lax.rem(z + nz - step, nz)

    barrier = pltpu.get_barrier_semaphore()
    pl.semaphore_signal(barrier, inc=1, device_id=(r, z * 2 + other), device_id_type=MESH)
    for step in range(1, nr):
        pl.semaphore_signal(barrier, inc=1, device_id=(row_peer(step)[0], c), device_id_type=MESH)
    for step in range(1, nz):
        pl.semaphore_signal(
            barrier, inc=1, device_id=(r, z_peer(step)[0] * 2 + core), device_id_type=MESH
        )

    live = [counts[0, 0] > slot for slot in range(slots)]
    spot_i = [jnp.clip(places[0, 0, slot, 0], 0, tiles_i - 1) for slot in range(slots)]
    spot_j = [jnp.clip(places[0, 0, slot, 1], 0, tiles_j - 1) for slot in range(slots)]

    def weights(spot, tiles):
        return [
            [
                jnp.where(jnp.logical_and(live[slot], spot[slot] == at), 1.0, 0.0).astype(F32)
                for at in range(tiles)
            ]
            for slot in range(slots)
        ]

    w_i = weights(spot_i, tiles_i)
    w_j = weights(spot_j, tiles_j)

    spot_k = [jnp.clip(places[0, 0, slot, 2], 0, nr * spots - 1) for slot in range(slots)]
    number = lax.broadcasted_iota(jnp.int32, tags.shape[2:], 0)
    tag = jnp.full(tags.shape[2:], -1.0, F32)
    for slot in range(slots):
        mark = jnp.where(live[slot], spot_k[slot], -1).astype(F32)
        tag = jnp.where(number == slot, mark, tag)
    tags[core, r] = tag

    loads[0].wait()
    state_b = init_b[...]
    b_all[0][r] = state_b.astype(BF16)
    loads[1].wait()
    state_a = init_a[...]
    a_all[0][core, z] = state_a.astype(BF16)

    pl.semaphore_wait(barrier, 1 + (nr - 1) + (nz - 1))

    def send_b(s):
        return [push(b_all[s].at[r], b_all[s].at[r], row_peer(step)[0], c) for step in range(1, nr)]

    def send_a(s):
        mine_a = a_all[s].at[core, z]
        return [push(mine_a, mine_a, r, z_peer(step)[0] * 2 + core) for step in range(1, nz)]

    def pass_on(ref, far):
        done(far)
        return to_core(ref, ref)

    def spread_row(ref_at):
        return [push(ref_at(r), ref_at(r), row_peer(step)[0], c) for step in range(1, nr)]

    def spread_c(ref_at):
        if nzc == 1:
            return []
        return [
            push(ref_at(z), ref_at(z), r, z_peer(step)[0] * 2 + core) for step in range(1, nz)
        ]

    def done(copies):
        for copy in copies:
            copy.wait_recv()

    def total(ref, s, count):
        value = ref[s, 0]
        for at in range(1, count):
            value = value + ref[s, at]
        return value

    def turn(slot):
        def one(k, carry):
            flip[slot, k] = bricks[slot, k].T
            return carry
        lax.fori_loop(0, depth, one, 0, unroll=4)

    def tile_a(s, slot):
        half = qa // 2
        sides = [a_all[s][side, pl.ds(spot_i[slot] * half, half)] for side in range(2)]
        return jnp.stack(sides, axis=1).reshape(tile, rank)

    def tile_b(s, slot):
        return b_all[s][pl.ds(spot_j[slot] * qb, qb)].reshape(tile, rank)

    def rows_c(s, slot):
        at = spot_k[slot]
        within = lax.rem(at, spots)
        low = lax.rem(within, spots // 2)
        wide_c = c_all[s][lax.div(within, spots // 2), lax.div(at, spots)]
        flat = wide_c.astype(F32).reshape(spots // 2, depth, rank)
        picked = jnp.zeros((depth, rank), F32)
        for one in range(spots // 2):
            picked = picked + flat[one] * jnp.where(low == one, 1.0, 0.0).astype(F32)
        return picked

    strip = 8
    batch = 4

    def fill(wide, value_at, right):
        for k in range(0, depth, batch):
            wide[k * tile:(k + batch) * tile, :] = jnp.dot(
                value_at(k).reshape(batch * tile, tile), right, preferred_element_type=F32
            )

    def weigh(wide, c_rows, result):
        def body(at, carry):
            low = pl.multiple_of(at * strip, strip)
            sums = jnp.zeros((strip, rank), F32)
            for k in range(depth):
                part = wide[pl.ds(pl.multiple_of(k * tile + low, strip), strip), :]
                sums = sums + part * c_rows[k:k + 1]
            result[pl.ds(low, strip), :] = sums
            return carry

        lax.fori_loop(0, tile // strip, body, 0)

    def along_c(s, slot):
        wide = deep_all.at[slot]
        acc_b[slot] = tile_b(s, slot).astype(F32)

        def body(at, carry):
            low = pl.multiple_of(at * strip, strip)
            rows = acc_b[slot, pl.ds(low, strip), :]
            return tuple(
                carry[k] + wide[pl.ds(pl.multiple_of(k * tile + low, strip), strip), :] * rows
                for k in range(depth)
            )

        empty = tuple(jnp.zeros((strip, rank), F32) for _ in range(depth))
        found = lax.fori_loop(0, tile // strip, body, empty)
        cc[s, core, r, slot * depth:(slot + 1) * depth, :] = jnp.concatenate(
            [jnp.sum(one, axis=0, keepdims=True) for one in found], axis=0
        )

    def wide_stage(s):
        for slot in range(slots):
            fill(spread, lambda k: bricks[slot, k:k + batch], tile_b(s, slot))
            weigh(spread, rows_c(s, slot), acc_a.at[slot])
        for g in range(nc):
            at, off = g // qa, (g % qa) * ra
            da[s, g % 2, g // 2] = sum(
                w_i[slot][at] * acc_a[slot, off:off + ra, :] for slot in range(slots)
            )
        return to_core(da.at[s, other], da1.at[s])

    def deep_stage(s):
        for slot in range(slots):
            fill(deep_all.at[slot], lambda k: flip[slot, k:k + batch], tile_a(s, slot))
            along_c(s, slot)
        return spread_row(lambda at: cc.at[s, core, at])

    def drive_b_stage(s):
        for slot in range(slots):
            weigh(deep_all.at[slot], rows_c(s, slot), acc_b.at[slot])
        for g in range(nr):
            at, off = g // qb, (g % qb) * rb
            db[s, g] = sum(
                w_j[slot][at] * acc_b[slot, off:off + rb, :] for slot in range(slots)
            )
        db2[s, r] = db[s, r]
        return [
            push(db.at[s, row_peer(step)[0]], db2.at[s, r], row_peer(step)[0], c)
            for step in range(1, nr)
        ]

    def drive_a_stage(s, arriving):
        copies = []
        arriving.wait_recv()
        for step in list(range(1, nz)) + [0]:
            to = z_peer(step)[0]
            if step == 0:
                da2[s, z] = da[s, core, z] + da1[s, z]
            else:
                da_sum[s, to] = da[s, core, to] + da1[s, to]
                copies.append(push(da_sum.at[s, to], da2.at[s, z], r, to * 2 + core))
        return copies

    def drive_c_stage(s):
        half = spots // 2
        found = []
        for one in range(half):
            want = (r * spots + core * half + one).astype(F32)
            sums = jnp.zeros((depth, rank), F32)
            for src in range(nr):
                for side in range(2):
                    for slot in range(slots):
                        term = cc[s, side, src, slot * depth:(slot + 1) * depth, :]
                        mark = tags[side, src, slot:slot + 1, :]
                        sums = sums + jnp.where(mark == want, term, 0.0)
            found.append(sums)
        csum[s] = jnp.concatenate(found, axis=0).reshape(csum.shape[1:])
        c3[s, z] = csum[s, mine]
        copies = []
        for step in range(1, nz):
            to = z_peer(step)[0]
            copies.append(
                push(csum.at[s, to if nzc > 1 else 0], c3.at[s, z], r, to * 2 + core)
            )
        return copies

    def gram_b_stage(s):
        sb_part[s] = gram(b_all[s][...].reshape(nr * rb, rank)).reshape(sb_part.shape[1:])
        return to_core(sb_part.at[s, r, other], sb1.at[s])

    def pair_b_stage(s, arriving):
        arriving.wait_recv()
        sb2[s, z] = sb_part[s, r, core] + sb1[s]
        return [
            push(sb2.at[s, z], sb2.at[s, z], r, z_peer(step)[0] * 2 + core)
            for step in range(1, nz)
        ]

    def gram_a_stage(s):
        sa_part[s] = gram(a_all[s][...].reshape(nc * ra, rank)).reshape(sa_part.shape[1:])
        sa1[s, r] = sa_part[s, core, r]
        return [
            push(sa_part.at[s, core, row_peer(step)[0]], sa1.at[s, r], row_peer(step)[0], c)
            for step in range(1, nr)
        ]

    def prepare(state, hess):
        scale = jnp.sum(jnp.abs(hess), axis=0, keepdims=True) + 1e-06
        high = hess.astype(BF16)
        low = (hess - high.astype(F32)).astype(BF16)
        top = state.astype(BF16)
        rest = (state - top.astype(F32)).astype(BF16)
        rows = state.shape[0]
        both = jnp.dot(
            jnp.concatenate([top, rest], axis=0), high, preferred_element_type=F32
        )
        moved = both[:rows] + both[rows:] + jnp.dot(top, low, preferred_element_type=F32)
        return moved, scale

    def finish(state, ready, drive, rate):
        moved, scale = ready
        return state - rate * (moved - drive) / scale

    far_b = send_b(0)
    far_a = send_a(0)
    far_tags = spread_row(lambda at: tags.at[core, at])
    loads[2].wait()
    mine = z if nzc > 1 else 0
    start_c = r * k_row + core * k_half + mine * (k_half // nzc)
    state_c = init_c[pl.ds(pl.multiple_of(start_c, 8), k_half // nzc), :]
    for at in range(nr):
        for side in range(2):
            low = at * k_row + side * k_half
            c_all[0][side, at] = init_c[low:low + k_half, :].astype(BF16).reshape(
                c_all[0].shape[2:]
            )
    gram_c = gram(c_all[0][...].reshape(nr * k_row, rank))
    loads[3].wait()
    for slot in range(slots):
        turn(slot)
    far_c = []

    for s in range(sweeps):
        last = s == sweeps - 1
        first = s == 0
        done(far_b)
        step_sb1 = gram_b_stage(s)
        if first:
            step_da1 = wide_stage(s)
        near_a = pass_on(a_all[s].at[core], far_a)
        step_sb2 = pair_b_stage(s, step_sb1)
        if first:
            step_da2 = drive_a_stage(s, step_da1)
        else:
            done(far_c)
            far_c = spread_row(lambda at: c_all[s].at[core, at])
        near_a.wait_recv()
        step_c1 = deep_stage(s)
        step_sa1 = gram_a_stage(s)
        if first:
            step_db = drive_b_stage(s)
            near_tags = pass_on(tags.at[core], far_tags)
        else:
            near_c = pass_on(c_all[s].at[core], far_c)
        near_cc = pass_on(cc.at[s, core], step_c1)
        if not first:
            near_c.wait_recv()
            step_da1 = wide_stage(s)
        done(step_sa1)
        sa_full[s, core, r] = total(sa1, s, nr)
        step_sa2 = spread_row(lambda at: sa_full.at[s, core, at])
        done(step_sb2)
        sb_full[s, core, r] = total(sb2, s, nz)
        step_sb3 = spread_row(lambda at: sb_full.at[s, core, at])
        if first:
            near_tags.wait_recv()
        near_cc.wait_recv()
        step_c3 = drive_c_stage(s)
        if not first:
            step_da2 = drive_a_stage(s, step_da1)
            gram_c = gram(c_all[s][...].reshape(nr * k_row, rank))
            step_db = drive_b_stage(s)
        near_sa = pass_on(sa_full.at[s, core], step_sa2)
        near_sb = pass_on(sb_full.at[s, core], step_sb3)
        near_sb.wait_recv()
        gram_b = jnp.stack([sb_full[s, side] for side in range(2)], axis=1).reshape(rank, rank)
        if not last:
            ready_a = prepare(state_a, gram_b * gram_c)
            done(step_da2)
            state_a = jnp.maximum(finish(state_a, ready_a, total(da2, s, nz), rates[s, 0]), 0.0)
            a_all[s + 1][core, z] = state_a.astype(BF16)
            far_a = send_a(s + 1)
            near_sa.wait_recv()
            gram_a = sa_full[s].reshape(rank, rank)
            ready_b = prepare(state_b, gram_a * gram_c)
            done(step_db)
            state_b = jnp.maximum(finish(state_b, ready_b, total(db2, s, nr), rates[s, 1]), 0.0)
            b_all[s + 1][r] = state_b.astype(BF16)
            far_b = send_b(s + 1)
            ready_c = prepare(state_c, gram_a * gram_b)
            done(step_c3)
            state_c = jnp.maximum(finish(state_c, ready_c, total(c3, s, nz), rates[s, 2]), 0.0)
            c_all[s + 1][core, r, mine] = state_c.astype(BF16)
            far_c = spread_c(lambda at: c_all[s + 1].at[core, r, at])
        else:
            near_sa.wait_recv()
            gram_a = sa_full[s].reshape(rank, rank)
            ready_c = prepare(state_c, gram_a * gram_b)
            done(step_c3)
            final_c[core, r, mine] = finish(state_c, ready_c, total(c3, s, nz), rates[s, 2])
            far_c = spread_c(lambda at: final_c.at[core, r, at])
            ready_b = prepare(state_b, gram_a * gram_c)
            ready_a = prepare(state_a, gram_b * gram_c)
            done(far_c)
            far_c = spread_row(lambda at: final_c.at[core, at])
            done(step_db)
            out_b[...] = finish(state_b, ready_b, total(db2, s, nr), rates[s, 1])
            done(step_da2)
            out_a[...] = finish(state_a, ready_a, total(da2, s, nz), rates[s, 0])
            near_c = pass_on(final_c.at[core], far_c)
            for at in range(nr):
                out_c[at, core] = final_c[core, at]
            near_c.wait_recv()
            for at in range(nr):
                out_c[at, other] = final_c[other, at]

    for copy in started:
        copy.wait_send()
    assert used[0] <= sems_of


def clamp(*arrays):
    count = len(arrays)

    def clamp_all(*refs):
        inner, outer, held, sems = refs[:count], refs[count:2 * count], refs[2 * count:-1], refs[-1]
        loads = [
            pltpu.make_async_copy(inner[at], held[at], sems.at[at]) for at in range(count)
        ]
        for load in loads:
            load.start()
        copies = []
        for at in range(count):
            loads[at].wait()
            held[at][...] = jnp.maximum(held[at][...], 0.0)
            copies.append(pltpu.make_async_copy(held[at], outer[at], sems.at[count + at]))
            copies[-1].start()
        for copy in copies:
            copy.wait()

    far = pl.BlockSpec(memory_space=pltpu.HBM)
    return pl.pallas_call(
        clamp_all,
        out_shape=tuple(jax.ShapeDtypeStruct(one.shape, one.dtype) for one in arrays),
        in_specs=[far] * count,
        out_specs=(far,) * count,
        scratch_shapes=[pltpu.VMEM(one.shape, one.dtype) for one in arrays]
        + [pltpu.SemaphoreType.DMA((2 * count,))],
        compiler_params=pltpu.CompilerParams(vmem_limit_bytes=VMEM_BYTES),
        name="clamp",
    )(*arrays)


def shards(nr, nc, bricks, brick_coords, brick_counts, step_sizes, init_a, init_b, init_c):
    slots, depth, tile, _ = bricks.shape[2:]
    sweeps = step_sizes.shape[0]
    ra, rank = init_a.shape[1:]
    rb = init_b.shape[1]
    depth_c = init_c.shape[0]
    nz = nc // 2
    k_row = depth_c // nr
    k_half = k_row // 2
    nzc = nz if k_half % (nz * 16) == 0 else 1
    rc = k_half // nzc
    tags = -(-slots // 8) * 8
    sems = 2 * nr + sweeps * (6 * nz + 13 * nr)
    smem = pl.BlockSpec(memory_space=pltpu.SMEM)
    far = pl.BlockSpec(memory_space=pltpu.HBM)
    vmem = pl.BlockSpec(memory_space=pltpu.VMEM)
    scratch = [
        ((slots, depth, tile, tile), BF16),
        ((ra, rank), F32),
        ((rb, rank), F32),
        ((depth_c, rank), F32),
        ((slots, depth, tile, tile), BF16),
        [((2, nz, ra, rank), BF16)] * sweeps,
        [((nr, rb, rank), BF16)] * sweeps,
        [((2, nr, nzc, rc, rank), BF16)] * sweeps,
        ((slots, tile, rank), F32),
        ((slots, tile, rank), F32),
        ((depth * tile, rank), F32),
        ((slots, depth * tile, rank), F32),
        ((2, nr, nzc, rc, rank), F32),
        ((sweeps, 2, nz, ra, rank), F32),
        ((sweeps, nz, ra, rank), F32),
        ((sweeps, nz, ra, rank), F32),
        ((sweeps, nz, ra, rank), F32),
        ((sweeps, nr, rb, rank), F32),
        ((sweeps, nr, rb, rank), F32),
        ((sweeps, 2, nr, slots * depth, rank), F32),
        ((2, nr, tags, rank), F32),
        ((sweeps, nzc, rc, rank), F32),
        ((sweeps, nz, rc, rank), F32),
        ((sweeps, 2, nr, rank // nr // 2, rank), F32),
        ((sweeps, nr, rank // nr // 2, rank), F32),
        ((sweeps, 2, nr, rank // nr // 2, rank), F32),
        ((sweeps, nr, 2, rank // nr // 2, rank), F32),
        ((sweeps, rank // nr // 2, rank), F32),
        ((sweeps, nz, rank // nr // 2, rank), F32),
        ((sweeps, 2, nr, rank // nr // 2, rank), F32),
    ]
    new_a, new_b, new_c = pl.pallas_call(
        functools.partial(kernel, nr, nc, sems),
        out_shape=(
            jax.ShapeDtypeStruct((ra, rank), F32),
            jax.ShapeDtypeStruct((rb, rank), F32),
            jax.ShapeDtypeStruct((nr, 2, nzc, rc, rank), F32),
        ),
        in_specs=[smem, smem, smem] + [far] * 4,
        out_specs=(vmem, vmem, vmem),
        scratch_shapes=[
            [pltpu.VMEM(*each) for each in one] if isinstance(one, list) else pltpu.VMEM(*one)
            for one in scratch
        ]
        + [pltpu.SemaphoreType.DMA((4,)), pltpu.SemaphoreType.DMA((sems,)), pltpu.SemaphoreType.DMA((sems,))],
        compiler_params=pltpu.CompilerParams(
            collective_id=0, has_side_effects=True, vmem_limit_bytes=VMEM_BYTES
        ),
        name="sweeps",
    )(
        jnp.swapaxes(brick_coords, 2, 3), brick_counts, step_sizes,
        bricks.reshape(slots, depth, tile, tile), init_a[0], init_b[0], init_c,
    )
    last_a, last_b, last_c = clamp(new_a, new_b, new_c.reshape(depth_c, rank))
    return last_a[None], last_b[None], last_c


def solution(mesh):
    placed = (
        P("row", "col", None, None, None, None),
        P("row", "col", None, None),
        P("row", "col"),
        P(),
        P("row", "col", None),
        P("col", "row", None),
        P(),
    )
    return jax.shard_map(
        functools.partial(shards, mesh.shape["row"], mesh.shape["col"]),
        mesh=mesh,
        in_specs=placed,
        out_specs=(P("row", "col", None), P("col", "row", None), P()),
        check_vma=False,
    )
```
